512 devices in a mesh: dp: 8 (over z_lo), ctx: 8 (over z_hi, x), head: 8 (over y, core).
Axes of the slice: x: 4, y: 4, z: 16 (z_hi: 2, z_lo: 8; z = z_hi * 8 + z_lo), core: 2. Of those that a mesh axis runs over, the one named last changes fastest.
Arguments:
- queries: bfloat16 [8, 1024, 2048], P('dp', 'ctx', 'head')
- keyval: bfloat16 [8, 2, 1024, 1024], P('dp', None, 'ctx', 'head')
- attn_grad: bfloat16 [8, 1024, 2048], P('dp', 'ctx', 'head'), may hold values from -6 to 6
- doc_ids: int32 [8, 1024], P('dp', 'ctx'), may hold values from 0 to 3, never falling along the last dimension, each value on 1 to 512 neighbouring positions
- ssm_in: bfloat16 [8, 1024, 8192], P('dp', 'ctx', 'head'), may hold values from -6 to 6
- bc_pair: bfloat16 [8, 2, 1024, 128], P('dp', None, 'ctx'), may hold values from -0.625 to 0.625
- step_size: float32 [8, 128, 1024], P('dp', 'head', 'ctx'), as said below
- decay_rate: float32 [128], P('head'), may hold values from 0.5 to 2
- skip_gain: float32 [128], P('head'), may hold values from 0.5 to 1.5
- ssm_grad: bfloat16 [8, 1024, 8192], P('dp', 'ctx', 'head'), may hold values from -6 to 6
Outputs:
- query_grad: bfloat16 [8, 1024, 2048], P('dp', 'ctx', 'head')
- keyval_grad: bfloat16 [8, 2, 1024, 1024], P('dp', None, 'ctx', 'head')
- input_grad: bfloat16 [8, 1024, 8192], P('dp', 'ctx', 'head')
- shared_grad: float32 [8, 2, 1024, 128], P('dp', None, ('ctx', 'head'))
- step_grad: float32 [8, 128, 1024], P('dp', 'head', 'ctx')
- param_grads: float32 [2, 128], P(None, 'head')
The draws below stay inside these ranges and needn't reach their ends.
Inputs may be any that keep to these rules, and one draw needn't show every extreme that they name: `step_size`: positive. `doc_ids`: document numbers of each sequence never fall; a document holds at most 512 positions and one holds exactly 512.
All inputs are finite; a program needn't handle non-finite values.
Results may differ from the reference program's by a relative error of at most 0.017.
Values may be sent and summed in bfloat16 or wider, within the bound.
No kernel may reach another device: no remote copies, remote signals or barrier semaphores. Data moves between devices by JAX's collectives and lax.ppermute only.
A program may use at most 64 MiB of HBM per device.

```python
import math
import jax
import jax.numpy as jnp
import numpy as np
from jax import lax

TOK_DEV = 128
HEAD_WIDTH = 128
QUERY_PER_KV = 2
PD = 64
NS = 128
DOCS = 4
SEQUENCE_COUNT = 8
SEQUENCE_LENGTH = 1024
MOST = 512
HQ = 16
KEYVALUE_HEADS = 8
HS = 128


def attention_inputs(key):
    baseline_tensor = jax.random.normal(jax.random.fold_in(key, 11), (SEQUENCE_COUNT, SEQUENCE_LENGTH, KEYVALUE_HEADS, HEAD_WIDTH), jnp.float32)
    value_tensor = jax.random.normal(jax.random.fold_in(key, 13), (SEQUENCE_COUNT, SEQUENCE_LENGTH, KEYVALUE_HEADS, HEAD_WIDTH), jnp.float32)
    simple_tensor = jax.random.normal(jax.random.fold_in(key, 14), (SEQUENCE_COUNT, SEQUENCE_LENGTH, KEYVALUE_HEADS, QUERY_PER_KV, HEAD_WIDTH), jnp.float32)
    keys = baseline_tensor
    queries = simple_tensor
    return (queries, keys, value_tensor)


def draw_queries(key, part):
    queries = attention_inputs(key)[0]
    return queries.reshape(SEQUENCE_COUNT, SEQUENCE_LENGTH, KEYVALUE_HEADS * QUERY_PER_KV * HEAD_WIDTH).astype(jnp.bfloat16)


def draw_keyval(key, part):
    outputs = attention_inputs(key)
    stacked_tensors = jnp.stack([outputs[1], outputs[2]], axis=1)
    return stacked_tensors.reshape(SEQUENCE_COUNT, 2, SEQUENCE_LENGTH, KEYVALUE_HEADS * HEAD_WIDTH).astype(jnp.bfloat16)


def draw_step_size(key, part):
    key = jax.random.fold_in(key, 3)
    share = 0.5
    fast = jax.random.uniform(jax.random.fold_in(key, 1), (SEQUENCE_COUNT, HS, 1)) < share
    baseline_tensor = jnp.where(fast, 0.04, 0.5 / SEQUENCE_LENGTH)
    coarse_tensor = jax.random.uniform(jax.random.fold_in(key, 2), (SEQUENCE_COUNT, HS, SEQUENCE_LENGTH), minval=0.5, maxval=1.5)
    spike_samples = jax.random.randint(jax.random.fold_in(key, 4), (SEQUENCE_COUNT, 1, 2, 1), 0, SEQUENCE_LENGTH)
    spike_sample = jnp.any(spike_samples == jnp.arange(SEQUENCE_LENGTH)[None, None, None, :], axis=2)
    return (baseline_tensor * coarse_tensor + 0.3 * spike_sample.astype(jnp.float32)).astype(jnp.float32)


def shard_levels(key, shape, cuts, least, top_value):
    level = 1.0
    for position, shards_of in cuts:
        steps = jax.random.uniform(jax.random.fold_in(jax.random.fold_in(key, 6), position), (shards_of,), jnp.float32, least / len(cuts), top_value / len(cuts))
        level = level * jnp.repeat(jnp.exp(steps), shape[position] // shards_of).reshape((-1,) + (1,) * (len(shape) - 1 - position))
    return level


def split_up(amount, total, bound, slope):
    loads = [(1 << 20) // math.isqrt(standing ** slope) + 1 for standing in range(2, amount + 1)]
    surplus, given = total - bound - (amount - 1), [1] * (amount - 1)
    while surplus > 0:
        free = [i for i in range(amount - 1) if given[i] < bound]
        whole, remaining = sum([loads[i] for i in free]), surplus
        for i in free:
            more = min(bound - given[i], max(1, remaining * loads[i] // whole), surplus)
            given[i] = given[i] + more
            surplus = surplus - more
    return np.array([bound] + given)


def uneven(rng, number_of, total, bound, skew):
    if number_of == 2:
        one = jax.random.randint(rng, (), max(1, total - bound), min(bound, total - 1) + 1)
        return jnp.stack([one, total - one])
    tallies = jnp.asarray(split_up(number_of, total, bound, skew), jnp.int32)
    twos = (number_of - 1) // 2
    source_of, receiver = tallies[1:1 + 2 * twos:2], tallies[2:2 + 2 * twos:2]
    margin = jnp.minimum(source_of - 1, bound - receiver)
    moved = jax.random.randint(jax.random.fold_in(rng, 1), (twos,), 0, 1 << 20) % (margin + 1)
    tallies = tallies.at[1:1 + 2 * twos:2].set(source_of - moved).at[2:2 + 2 * twos:2].set(receiver + moved)
    return tallies[jax.random.permutation(jax.random.fold_in(rng, 2), number_of)]


def centred(stream_key, dims, scale, bound, split=(), held_as=jnp.bfloat16):
    values = scale * jax.random.normal(stream_key, dims, jnp.float32)
    if split:
        values = values * shard_levels(stream_key, dims, split, -0.22, 0.18)
    return jnp.clip(values, -bound, bound).astype(held_as)


def setup_inputs(seed: int = 0) -> dict:
    seeds = jax.random.split(jax.random.key(seed), 11)
    return {
        "queries": draw_queries(jax.random.fold_in(seeds[10], 71), 0),
        "keyval": draw_keyval(jax.random.fold_in(seeds[10], 71), 0),
        "attn_grad": centred(seeds[2], (SEQUENCE_COUNT, SEQUENCE_LENGTH, HQ * HEAD_WIDTH), 1.0, 6.0, ((0, 8), (1, 8), (2, 8))),
        "doc_ids": jax.vmap(lambda own: jnp.searchsorted(jnp.cumsum(uneven(own, DOCS, SEQUENCE_LENGTH, MOST, 0)), jnp.arange(SEQUENCE_LENGTH), side="right"))(jax.random.split(seeds[3], SEQUENCE_COUNT)).reshape((SEQUENCE_COUNT, SEQUENCE_LENGTH)).astype(jnp.int32),
        "ssm_in": centred(seeds[4], (SEQUENCE_COUNT, SEQUENCE_LENGTH, HS * PD), 1.0, 6.0, ((0, 8), (1, 8), (2, 8))),
        "bc_pair": centred(seeds[5], (SEQUENCE_COUNT, 2, SEQUENCE_LENGTH, NS), (0.5 * NS ** -0.5), 0.625, ((0, 8), (2, 8))),
        "step_size": draw_step_size(jax.random.fold_in(seeds[10], 71), 0),
        "decay_rate": jnp.clip(jnp.exp(math.log(2.0) - 1.3862944 * jax.random.uniform(seeds[7], (HS,), jnp.float32) ** shard_levels(seeds[7], (HS,), ((0, 8),), -0.2, 0.2)), 0.5, 2.0),
        "skip_gain": jnp.clip(0.5 + 1.0 * jax.random.uniform(seeds[8], (HS,), jnp.float32) ** shard_levels(seeds[8], (HS,), ((0, 8),), -0.2, 0.2), 0.5, 1.5),
        "ssm_grad": centred(seeds[9], (SEQUENCE_COUNT, SEQUENCE_LENGTH, HS * PD), 1.0, 6.0, ((0, 8), (1, 8), (2, 8))),
    }


HIGHEST_PRECISION = lax.Precision.HIGHEST
NEGATIVE = -1e+30

def attend_head(query_rows, key_rows, value_rows, grad_rows, documents):
    scaling = HEAD_WIDTH ** (-0.5)
    length = documents.shape[0]
    places = jnp.arange(length)
    allowed = (places[None, :] <= places[:, None]) & (documents[None, :] == documents[:, None])
    scores = jnp.einsum('gie,je->gij', query_rows.astype(jnp.float32), key_rows.astype(jnp.float32)) * scaling
    masked = jnp.where(allowed[None], scores, NEGATIVE)
    row_max = lax.optimization_barrier(jnp.max(masked, axis=-1, keepdims=True))
    row_sum = lax.optimization_barrier(jnp.sum(jnp.where(allowed[None], jnp.exp(masked - row_max), 0.0), axis=-1, keepdims=True))
    logsum = row_max + jnp.log(row_sum)
    dot_grads = jnp.einsum('gie,je->gij', grad_rows.astype(jnp.float32), value_rows.astype(jnp.float32))
    attention = jnp.where(allowed[None], jnp.exp(masked - logsum), 0.0)
    row_delta = lax.optimization_barrier(jnp.sum(attention * dot_grads, axis=-1, keepdims=True))
    rounded = attention.astype(jnp.bfloat16)
    dscore = (rounded.astype(jnp.float32) * (dot_grads - row_delta)).astype(jnp.bfloat16)
    query_grad = jnp.einsum('gij,je->gie', dscore.astype(jnp.float32), key_rows.astype(jnp.float32)) * scaling
    key_gradient_out = jnp.einsum('gij,gie->je', dscore.astype(jnp.float32), query_rows.astype(jnp.float32)) * scaling
    value_gradient_out = jnp.einsum('gij,gie->je', rounded.astype(jnp.float32), grad_rows.astype(jnp.float32))
    return (query_grad, key_gradient_out, value_gradient_out)

def decay_terms(step_rows, doc_rows, doc_before, rate):
    number = doc_rows.shape[0]
    log_decay = -step_rows * rate[:, None]
    cumulative = jnp.cumsum(log_decay, axis=-1)
    ending = cumulative[:, -1]
    places = jnp.arange(number)
    joined = (places[None, :] <= places[:, None]) & (doc_rows[None, :] == doc_rows[:, None])
    spread = cumulative[:, :, None] - cumulative[:, None, :]
    weights = jnp.where(joined[None], jnp.exp(jnp.minimum(spread, 0.0)), 0.0)
    entering = jnp.where(doc_rows[None, :] == doc_before, jnp.exp(cumulative), 0.0)
    leaving = jnp.where(doc_rows[None, :] == doc_rows[-1], jnp.exp(ending[:, None] - cumulative), 0.0)
    through = (doc_rows[0] == doc_before) & (doc_rows[-1] == doc_rows[0])
    passage = jnp.where(through, jnp.exp(ending), 0.0)
    return (weights, entering, leaving, passage)

def block_states(entries):
    inputs, writes, reads, out_grads, step_rows, doc_rows, doc_before, rate = entries
    weights, entering, leaving, passage = decay_terms(step_rows, doc_rows, doc_before, rate)
    scaled_in = jnp.transpose(leaving)[:, :, None] * inputs.astype(jnp.float32)
    scaled_grad = jnp.transpose(entering)[:, :, None] * out_grads.astype(jnp.float32)
    closing = jnp.einsum('sn,shp->hnp', writes.astype(jnp.float32), scaled_in, precision=HIGHEST_PRECISION)
    opening = jnp.einsum('tn,thp->hnp', reads.astype(jnp.float32), scaled_grad, precision=HIGHEST_PRECISION)
    return (passage, closing, opening)

def block_grads(entries):
    inputs, writes, reads, out_grads, step_rows, doc_rows, doc_before, rate, skip, state_in, grad_in = entries
    weights, entering, leaving, passage = decay_terms(step_rows, doc_rows, doc_before, rate)
    inputs_wide = inputs.astype(jnp.float32)
    grads_wide = out_grads.astype(jnp.float32)
    write_wide = writes.astype(jnp.float32)
    read_wide = reads.astype(jnp.float32)
    number = doc_rows.shape[0]
    affinity = jnp.einsum('tn,sn->ts', read_wide, write_wide)
    pairing = jnp.einsum('thp,shp->hts', grads_wide, inputs_wide)
    mixing = weights * affinity[None]
    paired = weights * pairing
    back_state = jnp.einsum('sn,hnp->shp', write_wide, grad_in, precision=HIGHEST_PRECISION)
    forward_read = jnp.einsum('tn,hnp->thp', read_wide, state_in, precision=HIGHEST_PRECISION)
    input_grad = jnp.einsum('hts,thp->shp', mixing, grads_wide, precision=HIGHEST_PRECISION) + jnp.transpose(leaving)[:, :, None] * back_state + skip[None, :, None] * grads_wide
    scaled_in = jnp.transpose(leaving)[:, :, None] * inputs_wide
    scaled_grad = jnp.transpose(entering)[:, :, None] * grads_wide
    write_grad = jnp.einsum('hts,tn->sn', paired, read_wide, precision=HIGHEST_PRECISION) + jnp.einsum('shp,hnp->sn', scaled_in, grad_in, precision=HIGHEST_PRECISION)
    read_grad = jnp.einsum('hts,sn->tn', paired, write_wide, precision=HIGHEST_PRECISION) + jnp.einsum('thp,hnp->tn', scaled_grad, state_in, precision=HIGHEST_PRECISION)
    triple = paired * affinity[None]
    earlier = jnp.cumsum(triple, axis=2) - triple
    places = jnp.arange(number)
    inside = lax.optimization_barrier(jnp.sum(jnp.where((places[:, None] >= places[None, :])[None], earlier, 0.0), axis=1))
    enter_term = entering * jnp.transpose(lax.optimization_barrier(jnp.sum(forward_read * grads_wide, axis=-1)))
    leave_term = leaving * jnp.transpose(lax.optimization_barrier(jnp.sum(back_state * inputs_wide, axis=-1)))
    enter_sum = jnp.flip(jnp.cumsum(jnp.flip(enter_term, -1), -1), -1)
    leave_sum = jnp.cumsum(leave_term, -1) - leave_term
    across = passage * lax.optimization_barrier(jnp.sum(state_in * grad_in, axis=(1, 2)))
    log_grad = inside + enter_sum + leave_sum + across[:, None]
    step_grad = -rate[:, None] * log_grad
    rate_term = lax.optimization_barrier(jnp.sum(-step_rows * log_grad, axis=-1))
    skip_term = lax.optimization_barrier(jnp.sum(inputs_wide * grads_wide, axis=(0, 2)))
    return (input_grad, write_grad, read_grad, step_grad, rate_term, skip_term)

def ssm_sequence(inputs, pair, out_grads, steps_seq, documents, rate, skip):
    number = TOK_DEV
    blocks = SEQUENCE_LENGTH // number
    input_blocks = inputs.reshape(blocks, number, HS, PD)
    grad_blocks = out_grads.reshape(blocks, number, HS, PD)
    write_blocks = pair[0].reshape(blocks, number, NS)
    read_blocks = pair[1].reshape(blocks, number, NS)
    step_blocks = jnp.transpose(steps_seq.reshape(HS, blocks, number), (1, 0, 2))
    doc_blocks = documents.reshape(blocks, number)
    befores = jnp.concatenate([jnp.full((1,), -1, jnp.int32), doc_blocks[:-1, -1].astype(jnp.int32)])
    rates = jnp.broadcast_to(rate, (blocks, HS))
    skips = jnp.broadcast_to(skip, (blocks, HS))
    passages, closings, openings = lax.map(block_states, (input_blocks, write_blocks, read_blocks, grad_blocks, step_blocks, doc_blocks, befores, rates))
    zero_state = jnp.zeros((HS, NS, PD), jnp.float32)

    def forward(running, entries):
        passage, contribution = entries
        return (passage[:, None, None] * running + contribution, running)
    state_ins = lax.scan(forward, zero_state, (passages, closings))[1]
    grad_ins = lax.scan(forward, zero_state, (passages, openings), reverse=True)[1]
    input_grad, write_grad, read_grad, step_grad, rate_term, skip_term = lax.map(block_grads, (input_blocks, write_blocks, read_blocks, grad_blocks, step_blocks, doc_blocks, befores, rates, skips, state_ins, grad_ins))
    input_grad = input_grad.reshape(SEQUENCE_LENGTH, HS * PD).astype(jnp.bfloat16)
    shared = jnp.stack([write_grad.reshape(SEQUENCE_LENGTH, NS), read_grad.reshape(SEQUENCE_LENGTH, NS)])
    step_grad = jnp.transpose(step_grad, (1, 0, 2)).reshape(HS, SEQUENCE_LENGTH)
    return (input_grad, shared, step_grad, lax.optimization_barrier(jnp.sum(rate_term, axis=0)), lax.optimization_barrier(jnp.sum(skip_term, axis=0)))

def reference(queries, keyval, attn_grad, doc_ids, ssm_in, bc_pair, step_size, decay_rate, skip_gain, ssm_grad):

    def one_sequence(entries):
        query_by_position, paired_by_position, gradient_by_position, documents, input_seq, bc_seq, out_seq, steps_seq = entries
        query_by_head = jnp.transpose(query_by_position.reshape(SEQUENCE_LENGTH, KEYVALUE_HEADS, QUERY_PER_KV, HEAD_WIDTH), (1, 2, 0, 3))
        gradient_by_head = jnp.transpose(gradient_by_position.reshape(SEQUENCE_LENGTH, KEYVALUE_HEADS, QUERY_PER_KV, HEAD_WIDTH), (1, 2, 0, 3))
        paired_by_head = jnp.transpose(paired_by_position.reshape(2, SEQUENCE_LENGTH, KEYVALUE_HEADS, HEAD_WIDTH), (2, 0, 1, 3))

        def one_head(members):
            query_rows, pair_rows, grad_rows = members
            return attend_head(query_rows, pair_rows[0], pair_rows[1], grad_rows, documents)
        query_grad, key_gradient_out, value_gradient_out = lax.map(one_head, (query_by_head, paired_by_head, gradient_by_head))
        query_grad = jnp.transpose(query_grad, (2, 0, 1, 3)).reshape(SEQUENCE_LENGTH, HQ * HEAD_WIDTH).astype(jnp.bfloat16)
        paired_gradient = jnp.transpose(jnp.stack([key_gradient_out, value_gradient_out]), (0, 2, 1, 3)).reshape(2, SEQUENCE_LENGTH, KEYVALUE_HEADS * HEAD_WIDTH).astype(jnp.bfloat16)
        ssm_parts = ssm_sequence(input_seq, bc_seq, out_seq, steps_seq, documents, decay_rate, skip_gain)
        return (query_grad, paired_gradient) + ssm_parts
    query_grad, keyval_grad, input_grad, shared_grad, step_grad, rate_terms, skip_terms = lax.map(one_sequence, (queries, keyval, attn_grad, doc_ids, ssm_in, bc_pair, ssm_grad, step_size))
    param_grads = jnp.stack([lax.optimization_barrier(jnp.sum(rate_terms, axis=0)), lax.optimization_barrier(jnp.sum(skip_terms, axis=0))]) / math.sqrt(SEQUENCE_COUNT * SEQUENCE_LENGTH * PD)
    return (query_grad, keyval_grad, input_grad, shared_grad, step_grad, param_grads)
```

```python
import functools
import math

import jax
import jax.numpy as jnp
from jax import lax
from jax.experimental import pallas as pl
from jax.experimental.pallas import tpu as pltpu
from jax.sharding import PartitionSpec as P

TOK = 128
WIDTH = 128
PD = 64
NS = 128
SSM_DEV = 16
COLS = SSM_DEV * PD
SIDE = 4
GROUP_COLS = COLS // SIDE
WINDOW = 5 * TOK
META = 16
STATE_ROWS = 2 * NS + META
ATT_ROWS = 3 * TOK + META
NEGATIVE = -1e30
F32 = jnp.float32
BF16 = jnp.bfloat16

NN = (((1,), (0,)), ((), ()))
NT = (((1,), (1,)), ((), ()))
TN = (((0,), (0,)), ((), ()))


def dot(a, b, dims):
    return lax.dot_general(a, b, dims, preferred_element_type=F32)


def pieces(value, count):
    out = []
    for _ in range(count):
        part = value.astype(BF16)
        out.append(part)
        value = value - part.astype(F32)
    return out


def exact_right(value, fixed, dims, count=2):
    return sum(dot(part, fixed, dims) for part in pieces(value, count))


def exact_left(fixed, value, dims, count=2):
    return sum(dot(fixed, part, dims) for part in pieces(value, count))


def iota(shape, dim):
    return lax.broadcasted_iota(jnp.int32, shape, dim)


def head_table(rows=SSM_DEV):
    lanes, row = iota((rows, COLS), 1), iota((rows, COLS), 0)
    return jnp.where((lanes >= row * PD) & (lanes < (row + 1) * PD), 1.0, 0.0).astype(BF16)


def triangle(keep):
    return jnp.where(keep(iota((TOK, TOK), 0), iota((TOK, TOK), 1)), 1.0, 0.0).astype(BF16)


def head_column(ref):
    row = iota((SSM_DEV, TOK), 0)
    out = jnp.zeros((SSM_DEV, TOK), F32)
    for h in range(SSM_DEV):
        out = jnp.where(row == h, ref[h], out)
    return out


def decays(step, rate, docs):
    cumulative = exact_right(-step * rate, triangle(lambda s, t: s <= t), NN, 3)
    ending = cumulative[:, TOK - 1 :]
    entering = jnp.where(docs == docs[:, :1], jnp.exp(cumulative), 0.0)
    leaving = jnp.where(docs == docs[:, TOK - 1 :], jnp.exp(ending - cumulative), 0.0)
    return cumulative, ending, entering, leaving


def local_states(x_ref, dy_ref, bc_ref, step_ref, rate_ref, docs_ref, out_ref, sin_ref, sgr_ref):
    docs = docs_ref[...]
    table = head_table()
    _, ending, entering, leaving = decays(step_ref[0], head_column(rate_ref), docs)
    scaled_in = (exact_right(leaving, table, TN) * x_ref[0].astype(F32)).astype(BF16)
    scaled_grad = (exact_right(entering, table, TN) * dy_ref[0].astype(F32)).astype(BF16)
    sin_ref[...] = scaled_in
    sgr_ref[...] = scaled_grad
    closing = dot(bc_ref[0, 0], scaled_in, TN).astype(BF16)
    opening = dot(bc_ref[0, 1], scaled_grad, TN).astype(BF16)
    passing = pieces(jnp.broadcast_to(jnp.exp(ending), (SSM_DEV, META)), 2)
    high, low = (dot(part, table, TN) for part in passing)
    row = iota((META, GROUP_COLS), 0)
    wide_docs = jnp.concatenate([docs.astype(F32), jnp.zeros((1, GROUP_COLS - TOK), F32)], axis=1)
    for g in range(SIDE):
        at = slice(g * GROUP_COLS, (g + 1) * GROUP_COLS)
        out_ref[g, :NS] = closing[:, at]
        out_ref[g, NS : 2 * NS] = opening[:, at]
        meta = jnp.where(row == 1, high[:, at], jnp.where(row == 2, low[:, at], 0.0))
        out_ref[g, 2 * NS :] = jnp.where(row == 0, wide_docs, meta).astype(BF16)


def carried(ref, state_start, grad_start):
    first, last, through = [], [], []
    for p in range(SIDE):
        meta = ref[p, 2 * NS :].astype(F32)
        first.append(meta[:1, :1])
        last.append(meta[:1, TOK - 1 : TOK])
        through.append(jnp.where(first[p] == last[p], meta[1:2] + meta[2:3], 0.0))
    state_in, grad_in = [state_start], [grad_start]
    for p in range(SIDE):
        leaves = ref[p, :NS].astype(F32) + through[p] * state_in[p]
        if p < SIDE - 1:
            leaves = jnp.where(last[p] == first[p + 1], 1.0, 0.0) * leaves
        state_in.append(leaves)
    for p in range(SIDE - 1, -1, -1):
        leaves = ref[p, NS : 2 * NS].astype(F32) + through[p] * grad_in[0]
        if p > 0:
            leaves = jnp.where(first[p] == last[p - 1], 1.0, 0.0) * leaves
        grad_in.insert(0, leaves)
    return state_in, grad_in, first[0], last[-1]


def half_totals(half_ref, ref, out_ref):
    zero = jnp.zeros((NS, GROUP_COLS), F32)
    state_in, grad_in, first, last = carried(ref, zero, zero)
    upper = half_ref[0] > 0
    out_ref[:NS] = jnp.where(upper, grad_in[0], state_in[-1]).astype(BF16)
    edge = jnp.where(upper, first, last)
    out_ref[NS:] = jnp.broadcast_to(edge, (META, GROUP_COLS)).astype(BF16)


def entering_states(half_ref, ref, other_ref, out_ref):
    upper = half_ref[0] > 0
    first = ref[0, 2 * NS :].astype(F32)[:1, :1]
    last = ref[SIDE - 1, 2 * NS :].astype(F32)[:1, TOK - 1 : TOK]
    edge = other_ref[NS:].astype(F32)[:1, :1]
    meets = jnp.where(edge == jnp.where(upper, first, last), 1.0, 0.0)
    arrived = meets * other_ref[:NS].astype(F32)
    zero = jnp.zeros_like(arrived)
    state_in, grad_in, _, _ = carried(
        ref, jnp.where(upper, arrived, zero), jnp.where(upper, zero, arrived)
    )
    for p in range(SIDE):
        out_ref[p, :NS] = state_in[p].astype(BF16)
        out_ref[p, NS:] = grad_in[p + 1].astype(BF16)


def inside_shard(
    x_ref, dy_ref, bc_ref, step_ref, rate_ref, skip_ref, docs_ref, near_ref, shared_ref, log_ref
):
    docs = docs_ref[...]
    cumulative = decays(step_ref[0], head_column(rate_ref), docs)[0]
    log_decay = -step_ref[0] * head_column(rate_ref)
    cumulative_t = exact_left(triangle(lambda t, s: s <= t), log_decay, NT, 3)
    writes, reads = bc_ref[0, 0], bc_ref[0, 1]
    wide = jnp.broadcast_to(docs.astype(F32), (SSM_DEV, TOK)).astype(BF16)
    docs_t = dot(triangle(lambda t, s: s == t), wide, NT)[:, :1]
    source, target = iota((TOK, TOK), 0), iota((TOK, TOK), 1)
    joined = (source <= target) & (docs_t == docs.astype(F32))
    affinity = dot(writes, reads, NT)
    after = triangle(lambda u, t: u >= t)
    paired_sum = jnp.zeros((TOK, TOK), F32)
    for h in range(SSM_DEV):
        at = slice(h * PD, (h + 1) * PD)
        x, dy = x_ref[0, :, at], dy_ref[0, :, at]
        spread = cumulative[h : h + 1] - cumulative_t[:, h : h + 1]
        weights = jnp.where(joined, jnp.exp(jnp.minimum(spread, 0.0)), 0.0)
        paired = weights * dot(x, dy, NT)
        near_ref[:, at] = dot((weights * affinity).astype(BF16), dy, NN) + skip_ref[h] * dy.astype(
            F32
        )
        paired_sum = paired_sum + paired
        reaching = exact_right(paired * affinity, after, NN)
        log_ref[h : h + 1] = jnp.sum(
            jnp.where(source < target, reaching, 0.0), axis=0, keepdims=True
        )
    shared_ref[0] = exact_right(paired_sum, reads, NN)
    shared_ref[1] = exact_right(paired_sum, writes, TN)


def finish_ssm(
    peers,
    params_rows,
    in_ref,
    x_ref,
    dy_ref,
    bc_ref,
    step_ref,
    rate_ref,
    docs_ref,
    sin_ref,
    sgr_ref,
    near_ref,
    shared_ref,
    log_ref,
    dx_ref,
    step_grad_ref,
    share_ref,
    params_ref,
):
    docs = docs_ref[...]
    table = head_table()
    rate = head_column(rate_ref)
    step = step_ref[0]
    _, ending, entering, leaving = decays(step, rate, docs)
    leave_term = jnp.zeros((SSM_DEV, TOK), F32)
    enter_term = jnp.zeros((SSM_DEV, TOK), F32)
    across = jnp.zeros((SSM_DEV, 8), F32)
    skips = jnp.zeros((8, SSM_DEV), F32)
    write_grad, read_grad = shared_ref[0], shared_ref[1]
    for g in range(SIDE):
        at = slice(g * GROUP_COLS, (g + 1) * GROUP_COLS)
        part = table[:, at]
        state_in, grad_in = in_ref[g, :NS], in_ref[g, NS:]
        x, dy = x_ref[0, :, at].astype(F32), dy_ref[0, :, at].astype(F32)
        back = exact_right(leaving, part, TN) * dot(bc_ref[0, 0], grad_in, NN)
        ahead = exact_right(entering, part, TN) * dot(bc_ref[0, 1], state_in, NN)
        dx_ref[0, :, at] = (near_ref[:, at] + back).astype(BF16)
        leave_term += exact_left(part, back * x, NT)
        enter_term += exact_left(part, ahead * dy, NT)
        meeting = jnp.sum(state_in.astype(F32) * grad_in.astype(F32), axis=0, keepdims=True)
        across += exact_left(part, jnp.broadcast_to(meeting, (8, GROUP_COLS)), NT)
        skip = jnp.sum(x * dy, axis=0, keepdims=True)
        skips += exact_right(jnp.broadcast_to(skip, (8, GROUP_COLS)), part, NT, 3)
        write_grad += dot(sin_ref[:, at], grad_in, NT)
        read_grad += dot(sgr_ref[:, at], state_in, NT)
    through = jnp.where(docs[:, :1] == docs[:, TOK - 1 :], jnp.exp(ending), 0.0)
    log_grad = (
        log_ref[...]
        + exact_right(enter_term, triangle(lambda u, t: u >= t), NN)
        + exact_right(leave_term, triangle(lambda s, t: s < t), NN)
        + through * across[:, :1]
    )
    step_grad_ref[0] = -rate * log_grad
    rates = exact_left(jnp.ones((8, TOK), BF16), -step * log_grad, NT, 3)
    rows = TOK // peers
    for k in range(peers):
        at = slice(k * rows, (k + 1) * rows)
        share_ref[k, 0] = write_grad[at].astype(BF16)
        share_ref[k, 1] = read_grad[at].astype(BF16)
    both = jnp.concatenate(
        [rates[:1], skips[:1], jnp.zeros((1, TOK - 2 * SSM_DEV), F32)], axis=1
    )
    params_ref[...] = jnp.broadcast_to(both, (params_rows, TOK))


def attention(place_ref, in_ref, dq_ref, dkv_ref, key_scr, value_scr, doc_scr, total_scr):
    half, mine = place_ref[0], place_ref[1]
    scaling = WIDTH ** (-0.5)

    for j in range(2 * SIDE):
        which = lax.bitwise_xor(half, j // SIDE)
        rows = pl.ds(j * TOK, TOK)
        key_scr[rows] = in_ref[j % SIDE, which, 2 * TOK : 3 * TOK, :WIDTH]
        value_scr[rows] = in_ref[j % SIDE, which, 2 * TOK : 3 * TOK, WIDTH:]
        doc_scr[:, rows] = in_ref[j % SIDE, which, 3 * TOK :, :TOK].astype(F32)[:8]

    eye = triangle(lambda a, b: a == b)
    own_start = pl.multiple_of(mine * TOK, TOK)
    own_rows = pl.ds(own_start, TOK)
    own_keys, own_values = key_scr[own_rows], value_scr[own_rows]
    own_docs = doc_scr[:1, own_rows]
    key_lane = iota((TOK, WINDOW), 1)
    row_place = iota((TOK, WINDOW), 0)
    own_diff = iota((TOK, TOK), 1) - iota((TOK, TOK), 0)

    def rows_of(r, h):
        which = lax.bitwise_xor(half, r // SIDE)
        at = slice(h * WIDTH, (h + 1) * WIDTH)
        return in_ref[r % SIDE, which, :TOK, at], in_ref[r % SIDE, which, TOK : 2 * TOK, at]

    def shard(r, own):
        start = pl.multiple_of(jnp.maximum(r - SIDE, 0) * TOK, TOK)
        window = pl.ds(start, WINDOW)
        keys, values = key_scr[window], value_scr[window]
        row_docs = doc_scr[:, pl.ds(pl.multiple_of(r * TOK, TOK), TOK)].astype(BF16)
        docs_t = dot(eye, row_docs, NT)[:, :1]
        allowed = (key_lane + (start - r * TOK) <= row_place) & (docs_t == doc_scr[:1, window])
        own_allowed = (own_diff <= (r - mine) * TOK) & (docs_t == own_docs)
        for h in range(2):
            queries, grads = rows_of(r, h)
            scores = jnp.where(allowed, dot(queries, keys, NT) * scaling, NEGATIVE)
            top = jnp.max(scores, axis=1, keepdims=True)
            expos = jnp.where(allowed, jnp.exp(scores - top), 0.0)
            sums = jnp.sum(expos, axis=1, keepdims=True)
            dot_grads = dot(grads, values, NT)
            delta = jnp.sum(expos * dot_grads, axis=1, keepdims=True) / sums
            logsum = top + jnp.log(sums)
            if own:
                probs = jnp.where(allowed, jnp.exp(scores - logsum), 0.0).astype(BF16)
                dscore = (probs.astype(F32) * (dot_grads - delta)).astype(BF16)
                at = slice(h * WIDTH, (h + 1) * WIDTH)
                dq_ref[0, :, at] = (dot(dscore, keys, NN) * scaling).astype(BF16)
            scores = jnp.where(own_allowed, dot(queries, own_keys, NT) * scaling, NEGATIVE)
            probs = jnp.where(own_allowed, jnp.exp(scores - logsum), 0.0).astype(BF16)
            dot_grads = dot(grads, own_values, NT)
            dscore = (probs.astype(F32) * (dot_grads - delta)).astype(BF16)
            key_part = dot(dscore, queries, TN) * scaling
            value_part = dot(probs, grads, TN)
            if own and h == 0:
                total_scr[0] = key_part
                total_scr[1] = value_part
            else:
                total_scr[0] += key_part
                total_scr[1] += value_part

    shard(mine, True)
    lax.fori_loop(
        mine + 1,
        jnp.minimum(mine + SIDE, 2 * SIDE - 1) + 1,
        lambda r, _: (shard(r, False), 0)[1],
        0,
    )
    dkv_ref[0] = total_scr[...].astype(BF16)


def whole(count):
    return [pl.BlockSpec(memory_space=pltpu.VMEM)] * count


def scalars():
    return pl.BlockSpec(memory_space=pltpu.SMEM)


def params(megabytes=24):
    return pltpu.CompilerParams(vmem_limit_bytes=megabytes << 20)


def shape(dims, dtype):
    return jax.ShapeDtypeStruct(dims, dtype)


def body(
    queries, keyval, attn_grad, doc_ids, ssm_in, bc_pair, step_size, decay_rate, skip_gain, ssm_grad
):
    mine = lax.axis_index("ctx")
    half = mine // SIDE
    place = jnp.stack([half, mine]).astype(jnp.int32)
    peers = lax.axis_size("head")
    everyone = lax.axis_size("dp") * lax.axis_size("ctx")
    sides = [list(range(SIDE)), list(range(SIDE, 2 * SIDE))]
    across = [(i, i ^ SIDE) for i in range(2 * SIDE)]

    def between(value):
        return lax.all_to_all(value, "ctx", 0, 0, axis_index_groups=sides, tiled=True)

    docs_rows = jnp.broadcast_to(
        jnp.pad(doc_ids.astype(BF16), ((0, 0), (0, 2 * WIDTH - TOK))), (META, 2 * WIDTH)
    )
    attention_own = jnp.concatenate(
        [queries[0], attn_grad[0], jnp.concatenate([keyval[0, 0], keyval[0, 1]], axis=1), docs_rows]
    )
    attention_other = lax.ppermute(attention_own, "ctx", across)

    sent, scaled_in, scaled_grad = pl.pallas_call(
        local_states,
        out_shape=(
            shape((SIDE, STATE_ROWS, GROUP_COLS), BF16),
            shape((TOK, COLS), BF16),
            shape((TOK, COLS), BF16),
        ),
        in_specs=whole(4) + [scalars()] + whole(1),
        out_specs=tuple(whole(3)),
        compiler_params=params(),
        name="local_states",
    )(ssm_in, ssm_grad, bc_pair, step_size, decay_rate, doc_ids)
    received = between(sent)
    total = pl.pallas_call(
        half_totals,
        out_shape=shape((NS + META, GROUP_COLS), BF16),
        in_specs=[scalars()] + whole(1),
        out_specs=whole(1)[0],
        compiler_params=params(),
        name="half_totals",
    )(place, received)
    other_total = lax.ppermute(total, "ctx", across)

    step_after, _ = lax.optimization_barrier((step_size, total))
    near, shared_near, log_near = pl.pallas_call(
        inside_shard,
        out_shape=(
            shape((TOK, COLS), F32),
            shape((2, TOK, NS), F32),
            shape((SSM_DEV, TOK), F32),
        ),
        in_specs=whole(4) + [scalars(), scalars()] + whole(1),
        out_specs=tuple(whole(3)),
        compiler_params=params(),
        name="inside_shard",
        cost_estimate=pl.CostEstimate(flops=400 << 20, bytes_accessed=2 << 20, transcendentals=0),
    )(ssm_in, ssm_grad, bc_pair, step_after, decay_rate, skip_gain, doc_ids)

    own_after, _ = lax.optimization_barrier((attention_own, log_near))
    gathered = between(
        jnp.broadcast_to(
            jnp.stack([own_after, attention_other])[None], (SIDE, 2, ATT_ROWS, 2 * WIDTH)
        )
    )

    entering = pl.pallas_call(
        entering_states,
        out_shape=shape((SIDE, 2 * NS, GROUP_COLS), BF16),
        in_specs=[scalars()] + whole(2),
        out_specs=whole(1)[0],
        compiler_params=params(),
        name="entering_states",
    )(place, received, other_total)
    entered = between(entering)

    input_grad, step_grad, share, both = pl.pallas_call(
        functools.partial(finish_ssm, peers, everyone),
        out_shape=(
            shape((1, TOK, COLS), BF16),
            shape((1, SSM_DEV, TOK), F32),
            shape((peers, 2, TOK // peers, NS), BF16),
            shape((everyone, TOK), F32),
        ),
        in_specs=whole(5) + [scalars()] + whole(6),
        out_specs=tuple(whole(4)),
        compiler_params=params(),
        name="finish_ssm",
    )(
        entered,
        ssm_in,
        ssm_grad,
        bc_pair,
        step_size,
        decay_rate,
        doc_ids,
        scaled_in,
        scaled_grad,
        near,
        shared_near,
        log_near,
    )
    everywhere = lax.all_to_all(both, ("dp", "ctx"), 0, 0, tiled=True)
    shares = lax.all_to_all(share, "head", 0, 0, tiled=True)

    gathered, _ = lax.optimization_barrier((gathered, both))
    query_grad, keyval_grad = pl.pallas_call(
        attention,
        out_shape=(shape((1, TOK, 2 * WIDTH), BF16), shape((1, 2, TOK, WIDTH), BF16)),
        in_specs=[scalars()] + whole(1),
        out_specs=tuple(whole(2)),
        scratch_shapes=[
            pltpu.VMEM((2 * SIDE * TOK, WIDTH), BF16),
            pltpu.VMEM((2 * SIDE * TOK, WIDTH), BF16),
            pltpu.VMEM((8, 2 * SIDE * TOK), F32),
            pltpu.VMEM((2, TOK, WIDTH), F32),
        ],
        compiler_params=params(),
        name="attention",
        cost_estimate=pl.CostEstimate(flops=2 << 30, bytes_accessed=4 << 20, transcendentals=1 << 20),
    )(place, gathered)

    shared_grad = jnp.sum(shares.astype(F32), axis=0)[None]
    totals = jnp.sum(everywhere, axis=0)[: 2 * SSM_DEV].reshape(2, SSM_DEV)
    param_grads = totals / math.sqrt(lax.axis_size("dp") * lax.axis_size("ctx") * TOK * PD)
    return (query_grad, keyval_grad, input_grad, shared_grad, step_grad, param_grads)


def solution(mesh):
    placed = (
        P("dp", "ctx", "head"),
        P("dp", None, "ctx", "head"),
        P("dp", "ctx", "head"),
        P("dp", "ctx"),
        P("dp", "ctx", "head"),
        P("dp", None, "ctx", None),
        P("dp", "head", "ctx"),
        P("head"),
        P("head"),
        P("dp", "ctx", "head"),
    )
    return jax.shard_map(
        body,
        mesh=mesh,
        in_specs=placed,
        out_specs=(
            P("dp", "ctx", "head"),
            P("dp", None, "ctx", "head"),
            P("dp", "ctx", "head"),
            P("dp", None, ("ctx", "head"), None),
            P("dp", "head", "ctx"),
            P(None, "head"),
        ),
        check_vma=False,
    )
```

```python
import functools
import math

import jax
import jax.numpy as jnp
from jax import lax
from jax.experimental import pallas as pl
from jax.experimental.pallas import tpu as pltpu
from jax.sharding import PartitionSpec as P

TOK = 128
WIDTH = 128
PD = 64
NS = 128
SSM_DEV = 16
COLS = SSM_DEV * PD
SIDE = 4
GROUP_COLS = COLS // SIDE
WINDOW = 5 * TOK
META = 16
STATE_ROWS = 2 * NS + META
ATT_ROWS = 3 * TOK + META
NEGATIVE = -1e30
F32 = jnp.float32
BF16 = jnp.bfloat16

NN = (((1,), (0,)), ((), ()))
NT = (((1,), (1,)), ((), ()))
TN = (((0,), (0,)), ((), ()))


def dot(a, b, dims):
    return lax.dot_general(a, b, dims, preferred_element_type=F32)


def pieces(value, count):
    out = []
    for _ in range(count):
        part = value.astype(BF16)
        out.append(part)
        value = value - part.astype(F32)
    return out


def exact_right(value, fixed, dims, count=2):
    return sum(dot(part, fixed, dims) for part in pieces(value, count))


def exact_left(fixed, value, dims, count=2):
    return sum(dot(fixed, part, dims) for part in pieces(value, count))


def iota(shape, dim):
    return lax.broadcasted_iota(jnp.int32, shape, dim)


def head_table(rows=SSM_DEV):
    lanes, row = iota((rows, COLS), 1), iota((rows, COLS), 0)
    return jnp.where((lanes >= row * PD) & (lanes < (row + 1) * PD), 1.0, 0.0).astype(BF16)


def triangle(keep):
    return jnp.where(keep(iota((TOK, TOK), 0), iota((TOK, TOK), 1)), 1.0, 0.0).astype(BF16)


def head_column(ref):
    row = iota((SSM_DEV, TOK), 0)
    out = jnp.zeros((SSM_DEV, TOK), F32)
    for h in range(SSM_DEV):
        out = jnp.where(row == h, ref[h], out)
    return out


def decays(step, rate, docs):
    cumulative = exact_right(-step * rate, triangle(lambda s, t: s <= t), NN, 3)
    ending = cumulative[:, TOK - 1 :]
    entering = jnp.where(docs == docs[:, :1], jnp.exp(cumulative), 0.0)
    leaving = jnp.where(docs == docs[:, TOK - 1 :], jnp.exp(ending - cumulative), 0.0)
    return cumulative, ending, entering, leaving


def local_states(
    x_hbm,
    dy_hbm,
    bc_hbm,
    step_hbm,
    docs_hbm,
    rate_ref,
    out_ref,
    sin_ref,
    sgr_ref,
    x_ref,
    dy_ref,
    bc_ref,
    step_ref,
    docs_ref,
    arrived,
):
    pairs = ((step_hbm, step_ref), (docs_hbm, docs_ref), (x_hbm, x_ref), (bc_hbm, bc_ref))
    pairs += ((dy_hbm, dy_ref),)
    copies = [
        pltpu.make_async_copy(source, target, arrived.at[i])
        for i, (source, target) in enumerate(pairs)
    ]
    for copy in copies:
        copy.start()
    table = head_table()
    rate = head_column(rate_ref)
    copies[0].wait()
    copies[1].wait()
    docs = docs_ref[...]
    _, ending, entering, leaving = decays(step_ref[0], rate, docs)
    leaving, entering = exact_right(leaving, table, TN), exact_right(entering, table, TN)
    copies[2].wait()
    scaled_in = (leaving * x_ref[0].astype(F32)).astype(BF16)
    sin_ref[...] = scaled_in
    copies[3].wait()
    closing = dot(bc_ref[0, 0], scaled_in, TN).astype(BF16)
    copies[4].wait()
    scaled_grad = (entering * dy_ref[0].astype(F32)).astype(BF16)
    sgr_ref[...] = scaled_grad
    opening = dot(bc_ref[0, 1], scaled_grad, TN).astype(BF16)
    passing = pieces(jnp.broadcast_to(jnp.exp(ending), (SSM_DEV, META)), 2)
    high, low = (dot(part, table, TN) for part in passing)
    row = iota((META, GROUP_COLS), 0)
    wide_docs = jnp.concatenate([docs.astype(F32), jnp.zeros((1, GROUP_COLS - TOK), F32)], axis=1)
    for g in range(SIDE):
        at = slice(g * GROUP_COLS, (g + 1) * GROUP_COLS)
        out_ref[g, :NS] = closing[:, at]
        out_ref[g, NS : 2 * NS] = opening[:, at]
        meta = jnp.where(row == 1, high[:, at], jnp.where(row == 2, low[:, at], 0.0))
        out_ref[g, 2 * NS :] = jnp.where(row == 0, wide_docs, meta).astype(BF16)


def pack(queries_ref, grads_ref, keyval_ref, docs_ref, out_ref, pair_ref):
    out_ref[:TOK] = queries_ref[0]
    out_ref[TOK : 2 * TOK] = grads_ref[0]
    out_ref[2 * TOK : 3 * TOK, :WIDTH] = keyval_ref[0, 0]
    out_ref[2 * TOK : 3 * TOK, WIDTH:] = keyval_ref[0, 1]
    docs = jnp.broadcast_to(docs_ref[...].astype(F32), (META, TOK)).astype(BF16)
    out_ref[3 * TOK :, :WIDTH] = docs
    out_ref[3 * TOK :, WIDTH:] = docs
    pair_ref[...] = out_ref[2 * TOK :]


def carried(ref, state_start, grad_start):
    first, last, through = [], [], []
    for p in range(SIDE):
        meta = ref[p, 2 * NS :].astype(F32)
        first.append(meta[:1, :1])
        last.append(meta[:1, TOK - 1 : TOK])
        through.append(jnp.where(first[p] == last[p], meta[1:2] + meta[2:3], 0.0))
    state_in, grad_in = [state_start], [grad_start]
    for p in range(SIDE):
        leaves = ref[p, :NS].astype(F32) + through[p] * state_in[p]
        if p < SIDE - 1:
            leaves = jnp.where(last[p] == first[p + 1], 1.0, 0.0) * leaves
        state_in.append(leaves)
    for p in range(SIDE - 1, -1, -1):
        leaves = ref[p, NS : 2 * NS].astype(F32) + through[p] * grad_in[0]
        if p > 0:
            leaves = jnp.where(first[p] == last[p - 1], 1.0, 0.0) * leaves
        grad_in.insert(0, leaves)
    return state_in, grad_in, first[0], last[-1]


def half_totals(half_ref, ref, out_ref):
    zero = jnp.zeros((NS, GROUP_COLS), F32)
    state_in, grad_in, first, last = carried(ref, zero, zero)
    upper = half_ref[0] > 0
    out_ref[:NS] = jnp.where(upper, grad_in[0], state_in[-1]).astype(BF16)
    edge = jnp.where(upper, first, last)
    out_ref[NS:] = jnp.broadcast_to(edge, (META, GROUP_COLS)).astype(BF16)


def entering_states(half_ref, ref, other_ref, out_ref):
    upper = half_ref[0] > 0
    first = ref[0, 2 * NS :].astype(F32)[:1, :1]
    last = ref[SIDE - 1, 2 * NS :].astype(F32)[:1, TOK - 1 : TOK]
    edge = other_ref[NS:].astype(F32)[:1, :1]
    meets = jnp.where(edge == jnp.where(upper, first, last), 1.0, 0.0)
    arrived = meets * other_ref[:NS].astype(F32)
    zero = jnp.zeros_like(arrived)
    state_in, grad_in, _, _ = carried(
        ref, jnp.where(upper, arrived, zero), jnp.where(upper, zero, arrived)
    )
    for p in range(SIDE):
        out_ref[p, :NS] = state_in[p].astype(BF16)
        out_ref[p, NS:] = grad_in[p + 1].astype(BF16)


def inside_shard(
    x_ref, dy_ref, bc_ref, step_ref, rate_ref, skip_ref, docs_ref, near_ref, shared_ref, aux_ref
):
    docs = docs_ref[...]
    rate = head_column(rate_ref)
    cumulative, ending, entering, leaving = decays(step_ref[0], rate, docs)
    log_decay = -step_ref[0] * rate
    aux_ref[1] = entering
    aux_ref[2] = leaving
    through = jnp.where(docs[:, :1] == docs[:, TOK - 1 :], jnp.exp(ending), 0.0)
    aux_ref[3] = jnp.broadcast_to(through, (SSM_DEV, TOK))
    aux_ref[4] = -rate
    aux_ref[5] = -step_ref[0]
    skip = jnp.sum(x_ref[0].astype(F32) * dy_ref[0].astype(F32), axis=0, keepdims=True)
    lanes, row = iota((TOK, COLS), 1), iota((TOK, COLS), 0) - SSM_DEV
    later_table = jnp.where((lanes >= row * PD) & (lanes < (row + 1) * PD), 1.0, 0.0).astype(BF16)
    skips = exact_right(jnp.broadcast_to(skip, (SSM_DEV, COLS)), later_table, NT, 3)
    aux_ref[6] = skips
    cumulative_t = exact_left(triangle(lambda t, s: s <= t), log_decay, NT, 3)
    writes, reads = bc_ref[0, 0], bc_ref[0, 1]
    wide = jnp.broadcast_to(docs.astype(F32), (SSM_DEV, TOK)).astype(BF16)
    docs_t = dot(triangle(lambda t, s: s == t), wide, NT)[:, :1]
    source, target = iota((TOK, TOK), 0), iota((TOK, TOK), 1)
    joined = (source <= target) & (docs_t == docs.astype(F32))
    affinity = dot(writes, reads, NT)
    after = triangle(lambda u, t: u >= t)
    paired_sum = jnp.zeros((TOK, TOK), F32)
    for h in range(SSM_DEV):
        at = slice(h * PD, (h + 1) * PD)
        x, dy = x_ref[0, :, at], dy_ref[0, :, at]
        spread = cumulative[h : h + 1] - cumulative_t[:, h : h + 1]
        weights = jnp.where(joined, jnp.exp(jnp.minimum(spread, 0.0)), 0.0)
        paired = weights * dot(x, dy, NT)
        near_ref[:, at] = dot((weights * affinity).astype(BF16), dy, NN) + skip_ref[h] * dy.astype(
            F32
        )
        paired_sum = paired_sum + paired
        reaching = exact_right(paired * affinity, after, NN)
        aux_ref[0, h : h + 1] = jnp.sum(
            jnp.where(source < target, reaching, 0.0), axis=0, keepdims=True
        )
    shared_ref[0] = exact_right(paired_sum, reads, NN)
    shared_ref[1] = exact_right(paired_sum, writes, TN)


def finish_ssm(
    scale,
    in_ref,
    x_ref,
    dy_ref,
    bc_ref,
    near_ref,
    shared_ref,
    aux_ref,
    sin_ref,
    sgr_ref,
    dx_ref,
    step_grad_ref,
    share_ref,
    params_ref,
):
    table = head_table()
    entering, leaving = aux_ref[1], aux_ref[2]
    leave_term = jnp.zeros((SSM_DEV, TOK), F32)
    enter_term = jnp.zeros((SSM_DEV, TOK), F32)
    across = jnp.zeros((SSM_DEV, 8), F32)
    write_grad, read_grad = shared_ref[0], shared_ref[1]
    for g in range(SIDE):
        at = slice(g * GROUP_COLS, (g + 1) * GROUP_COLS)
        part = table[:, at]
        state_in, grad_in = in_ref[g, :NS], in_ref[g, NS:]
        x, dy = x_ref[0, :, at].astype(F32), dy_ref[0, :, at].astype(F32)
        back = exact_right(leaving, part, TN) * dot(bc_ref[0, 0], grad_in, NN)
        ahead = exact_right(entering, part, TN) * dot(bc_ref[0, 1], state_in, NN)
        dx_ref[0, :, at] = (near_ref[:, at] + back).astype(BF16)
        leave_term += exact_left(part, back * x, NT)
        enter_term += exact_left(part, ahead * dy, NT)
        meeting = jnp.sum(state_in.astype(F32) * grad_in.astype(F32), axis=0, keepdims=True)
        across += exact_left(part, jnp.broadcast_to(meeting, (8, GROUP_COLS)), NT)
        write_grad += dot(sin_ref[:, at], grad_in, NT)
        read_grad += dot(sgr_ref[:, at], state_in, NT)
    log_grad = (
        aux_ref[0]
        + exact_right(enter_term, triangle(lambda u, t: u >= t), NN)
        + exact_right(leave_term, triangle(lambda s, t: s < t), NN)
        + aux_ref[3] * across[:, :1]
    )
    step_grad_ref[0] = aux_ref[4] * log_grad
    rates = exact_left(jnp.ones((8, TOK), BF16), aux_ref[5] * log_grad, NT, 3)
    peers, _, rows, _ = share_ref.shape
    for k in range(peers):
        at = slice(k * rows, (k + 1) * rows)
        share_ref[k, 0] = write_grad[at].astype(BF16)
        share_ref[k, 1] = read_grad[at].astype(BF16)
    both = jnp.concatenate([rates[:1], jnp.zeros((1, TOK - SSM_DEV), F32)], axis=1)
    both = (both + aux_ref[6, :1]) * scale
    params_ref[...] = jnp.broadcast_to(both, params_ref.shape)


def attention(place_ref, *refs):
    dq_ref, dkv_ref, query_scr, grad_scr, key_scr, value_scr, doc_scr, total_scr = refs[SIDE:]
    half, mine = place_ref[0], place_ref[1]
    scaling = WIDTH ** (-0.5)

    for k in range(2):
        for step, ref in enumerate(refs[:SIDE]):
            shard_at = lax.bitwise_xor(half, k) * SIDE + lax.rem(mine + SIDE - step, SIDE)
            rows = pl.ds(pl.multiple_of(shard_at * TOK, TOK), TOK)
            query_scr[rows] = ref[k, :TOK]
            grad_scr[rows] = ref[k, TOK : 2 * TOK]
            key_scr[rows] = ref[k, 2 * TOK : 3 * TOK, :WIDTH]
            value_scr[rows] = ref[k, 2 * TOK : 3 * TOK, WIDTH:]
            doc_scr[:, rows] = ref[k, 3 * TOK :, :TOK].astype(F32)[:8]

    eye = triangle(lambda a, b: a == b)
    own_start = pl.multiple_of(mine * TOK, TOK)
    own_rows = pl.ds(own_start, TOK)
    own_keys, own_values = key_scr[own_rows], value_scr[own_rows]
    own_docs = doc_scr[:1, own_rows]
    key_lane = iota((TOK, WINDOW), 1)
    row_place = iota((TOK, WINDOW), 0)
    own_diff = iota((TOK, TOK), 1) - iota((TOK, TOK), 0)

    def rows_of(r, h):
        at, rows = slice(h * WIDTH, (h + 1) * WIDTH), pl.ds(pl.multiple_of(r * TOK, TOK), TOK)
        return query_scr[rows, at], grad_scr[rows, at]

    def shard(r, own):
        start = pl.multiple_of(jnp.maximum(r - SIDE, 0) * TOK, TOK)
        window = pl.ds(start, WINDOW)
        keys, values = key_scr[window], value_scr[window]
        row_docs = doc_scr[:, pl.ds(pl.multiple_of(r * TOK, TOK), TOK)].astype(BF16)
        docs_t = dot(eye, row_docs, NT)[:, :1]
        allowed = (key_lane + (start - r * TOK) <= row_place) & (docs_t == doc_scr[:1, window])
        own_allowed = (own_diff <= (r - mine) * TOK) & (docs_t == own_docs)
        for h in range(2):
            queries, grads = rows_of(r, h)
            scores = jnp.where(allowed, dot(queries, keys, NT) * scaling, NEGATIVE)
            top = jnp.max(scores, axis=1, keepdims=True)
            expos = jnp.where(allowed, jnp.exp(scores - top), 0.0)
            sums = jnp.sum(expos, axis=1, keepdims=True)
            dot_grads = dot(grads, values, NT)
            delta = jnp.sum(expos * dot_grads, axis=1, keepdims=True) / sums
            logsum = top + jnp.log(sums)
            if own:
                probs = jnp.where(allowed, jnp.exp(scores - logsum), 0.0).astype(BF16)
                dscore = (probs.astype(F32) * (dot_grads - delta)).astype(BF16)
                at = slice(h * WIDTH, (h + 1) * WIDTH)
                dq_ref[0, :, at] = (dot(dscore, keys, NN) * scaling).astype(BF16)
            scores = jnp.where(own_allowed, dot(queries, own_keys, NT) * scaling, NEGATIVE)
            probs = jnp.where(own_allowed, jnp.exp(scores - logsum), 0.0).astype(BF16)
            dot_grads = dot(grads, own_values, NT)
            dscore = (probs.astype(F32) * (dot_grads - delta)).astype(BF16)
            key_part = dot(dscore, queries, TN) * scaling
            value_part = dot(probs, grads, TN)
            if own and h == 0:
                total_scr[0] = key_part
                total_scr[1] = value_part
            else:
                total_scr[0] += key_part
                total_scr[1] += value_part

    shard(mine, True)
    lax.fori_loop(
        mine + 1,
        jnp.minimum(mine + SIDE, 2 * SIDE - 1) + 1,
        lambda r, _: (shard(r, False), 0)[1],
        0,
    )
    dkv_ref[0] = total_scr[...].astype(BF16)


def whole(count):
    return [pl.BlockSpec(memory_space=pltpu.VMEM)] * count


def scalars():
    return pl.BlockSpec(memory_space=pltpu.SMEM)


def params(megabytes=24):
    return pltpu.CompilerParams(vmem_limit_bytes=megabytes << 20)


def shape(dims, dtype):
    return jax.ShapeDtypeStruct(dims, dtype)


def body(
    queries, keyval, attn_grad, doc_ids, ssm_in, bc_pair, step_size, decay_rate, skip_gain, ssm_grad
):
    mine = lax.axis_index("ctx")
    half = mine // SIDE
    place = jnp.stack([half, mine]).astype(jnp.int32)
    peers = lax.axis_size("head")
    everyone = lax.axis_size("dp") * lax.axis_size("ctx")
    sides = [list(range(SIDE)), list(range(SIDE, 2 * SIDE))]
    across = [(i, i ^ SIDE) for i in range(2 * SIDE)]

    def between(value):
        return lax.all_to_all(value, "ctx", 0, 0, axis_index_groups=sides, tiled=True)

    sent, scaled_in, scaled_grad = pl.pallas_call(
        local_states,
        out_shape=(
            shape((SIDE, STATE_ROWS, GROUP_COLS), BF16),
            shape((TOK, COLS), BF16),
            shape((TOK, COLS), BF16),
        ),
        in_specs=[pl.BlockSpec(memory_space=pltpu.HBM)] * 5 + [scalars()],
        out_specs=tuple(whole(3)),
        scratch_shapes=[
            pltpu.VMEM(ssm_in.shape, BF16),
            pltpu.VMEM(ssm_grad.shape, BF16),
            pltpu.VMEM(bc_pair.shape, BF16),
            pltpu.VMEM(step_size.shape, F32),
            pltpu.VMEM(doc_ids.shape, jnp.int32),
            pltpu.SemaphoreType.DMA((5,)),
        ],
        compiler_params=params(63),
        name="local_states",
    )(ssm_in, ssm_grad, bc_pair, step_size, doc_ids, decay_rate)
    received = between(sent)

    docs_after, _ = lax.optimization_barrier((doc_ids, sent))
    own, own_pair = pl.pallas_call(
        pack,
        out_shape=(shape((ATT_ROWS, 2 * WIDTH), BF16), shape((TOK + META, 2 * WIDTH), BF16)),
        in_specs=whole(4),
        out_specs=tuple(whole(2)),
        compiler_params=params(),
        name="pack",
    )(queries, attn_grad, keyval, docs_after)
    from_above = lax.ppermute(own, "ctx", [(i + SIDE, i) for i in range(SIDE)])
    from_below = lax.ppermute(own_pair, "ctx", [(i, i + SIDE) for i in range(SIDE)])

    received, _ = lax.optimization_barrier((received, own))
    total = pl.pallas_call(
        half_totals,
        out_shape=shape((NS + META, GROUP_COLS), BF16),
        in_specs=[scalars()] + whole(1),
        out_specs=whole(1)[0],
        compiler_params=params(),
        name="half_totals",
    )(place, received)
    other_total = lax.ppermute(total, "ctx", across)

    def round_side(value, step):
        turn = [(i, (i & SIDE) | ((i + step) % SIDE)) for i in range(2 * SIDE)]
        return lax.ppermute(value, "ctx", turn)

    step_after, _ = lax.optimization_barrier((step_size, total))
    near, shared_near, aux = pl.pallas_call(
        inside_shard,
        out_shape=(
            shape((TOK, COLS), F32),
            shape((2, TOK, NS), F32),
            shape((7, SSM_DEV, TOK), F32),
        ),
        in_specs=whole(4) + [scalars(), scalars()] + whole(1),
        out_specs=tuple(whole(3)),
        compiler_params=params(),
        name="inside_shard",
        cost_estimate=pl.CostEstimate(flops=1 << 10, bytes_accessed=1 << 10, transcendentals=0),
    )(ssm_in, ssm_grad, bc_pair, step_after, decay_rate, skip_gain, doc_ids)

    received, aux, from_above, from_below = lax.optimization_barrier(
        (received, aux, from_above, from_below)
    )
    entering = pl.pallas_call(
        entering_states,
        out_shape=shape((SIDE, 2 * NS, GROUP_COLS), BF16),
        in_specs=[scalars()] + whole(2),
        out_specs=whole(1)[0],
        compiler_params=params(),
        name="entering_states",
    )(place, received, other_total)
    entered = between(entering)

    from_above, from_below, _ = lax.optimization_barrier((from_above, from_below, entering))
    other = from_above + jnp.pad(from_below, ((2 * TOK, 0), (0, 0)))
    halves = jnp.stack([own, other])
    shards = [halves] + [round_side(halves, step) for step in range(1, SIDE)]

    near, _ = lax.optimization_barrier((near, halves))
    scale = 1.0 / math.sqrt(everyone * TOK * PD)
    input_grad, step_grad, share, both = pl.pallas_call(
        functools.partial(finish_ssm, scale),
        out_shape=(
            shape((1, TOK, COLS), BF16),
            shape((1, SSM_DEV, TOK), F32),
            shape((peers, 2, TOK // peers, NS), BF16),
            shape((everyone, TOK), F32),
        ),
        in_specs=whole(9),
        out_specs=tuple(whole(4)),
        compiler_params=params(),
        name="finish_ssm",
    )(entered, ssm_in, ssm_grad, bc_pair, near, shared_near, aux, scaled_in, scaled_grad)
    shares = lax.all_to_all(share, "head", 0, 0, tiled=True)
    both, shares = lax.optimization_barrier((both, shares))
    everywhere = lax.all_to_all(both, ("dp", "ctx"), 0, 0, tiled=True)

    shards, _ = lax.optimization_barrier((shards, both))
    query_grad, keyval_grad = pl.pallas_call(
        attention,
        out_shape=(shape((1, TOK, 2 * WIDTH), BF16), shape((1, 2, TOK, WIDTH), BF16)),
        in_specs=[scalars()] + whole(SIDE),
        out_specs=tuple(whole(2)),
        scratch_shapes=[
            pltpu.VMEM((2 * SIDE * TOK, 2 * WIDTH), BF16),
            pltpu.VMEM((2 * SIDE * TOK, 2 * WIDTH), BF16),
            pltpu.VMEM((2 * SIDE * TOK, WIDTH), BF16),
            pltpu.VMEM((2 * SIDE * TOK, WIDTH), BF16),
            pltpu.VMEM((8, 2 * SIDE * TOK), F32),
            pltpu.VMEM((2, TOK, WIDTH), F32),
        ],
        compiler_params=params(),
        name="attention",
        cost_estimate=pl.CostEstimate(flops=2 << 30, bytes_accessed=4 << 20, transcendentals=1 << 20),
    )(place, *shards)

    everywhere, shares, query_grad = lax.optimization_barrier((everywhere, shares, query_grad))
    shared_grad = jnp.sum(shares.astype(F32), axis=0)[None]
    param_grads = jnp.sum(everywhere, axis=0)[: 2 * SSM_DEV].reshape(2, SSM_DEV)
    return (query_grad, keyval_grad, input_grad, shared_grad, step_grad, param_grads)


def solution(mesh):
    placed = (
        P("dp", "ctx", "head"),
        P("dp", None, "ctx", "head"),
        P("dp", "ctx", "head"),
        P("dp", "ctx"),
        P("dp", "ctx", "head"),
        P("dp", None, "ctx", None),
        P("dp", "head", "ctx"),
        P("head"),
        P("head"),
        P("dp", "ctx", "head"),
    )
    return jax.shard_map(
        body,
        mesh=mesh,
        in_specs=placed,
        out_specs=(
            P("dp", "ctx", "head"),
            P("dp", None, "ctx", "head"),
            P("dp", "ctx", "head"),
            P("dp", None, ("ctx", "head"), None),
            P("dp", "head", "ctx"),
            P(None, "head"),
        ),
        check_vma=False,
    )
```

```python
import functools
import math

import jax
import jax.numpy as jnp
from jax import lax
from jax.experimental import pallas as pl
from jax.experimental.pallas import tpu as pltpu
from jax.sharding import PartitionSpec as P

TOK = 128
WIDTH = 128
PD = 64
NS = 128
SSM_DEV = 16
COLS = SSM_DEV * PD
SIDE = 4
GROUP_COLS = COLS // SIDE
WINDOW = 5 * TOK
META = 16
STATE_ROWS = 2 * NS + META
ATT_ROWS = 3 * TOK + META
NEGATIVE = -1e30
F32 = jnp.float32
BF16 = jnp.bfloat16

NN = (((1,), (0,)), ((), ()))
NT = (((1,), (1,)), ((), ()))
TN = (((0,), (0,)), ((), ()))


def dot(a, b, dims):
    return lax.dot_general(a, b, dims, preferred_element_type=F32)


def pieces(value, count):
    out = []
    for _ in range(count):
        part = value.astype(BF16)
        out.append(part)
        value = value - part.astype(F32)
    return out


def exact_right(value, fixed, dims, count=2):
    return sum(dot(part, fixed, dims) for part in pieces(value, count))


def exact_left(fixed, value, dims, count=2):
    return sum(dot(fixed, part, dims) for part in pieces(value, count))


def iota(shape, dim):
    return lax.broadcasted_iota(jnp.int32, shape, dim)


def head_table(rows=SSM_DEV):
    lanes, row = iota((rows, COLS), 1), iota((rows, COLS), 0)
    return jnp.where((lanes >= row * PD) & (lanes < (row + 1) * PD), 1.0, 0.0).astype(BF16)


def triangle(keep):
    return jnp.where(keep(iota((TOK, TOK), 0), iota((TOK, TOK), 1)), 1.0, 0.0).astype(BF16)


def head_column(ref):
    row = iota((SSM_DEV, TOK), 0)
    out = jnp.zeros((SSM_DEV, TOK), F32)
    for h in range(SSM_DEV):
        out = jnp.where(row == h, ref[h], out)
    return out


def decays(step, rate, docs):
    cumulative = exact_right(-step * rate, triangle(lambda s, t: s <= t), NN, 3)
    ending = cumulative[:, TOK - 1 :]
    entering = jnp.where(docs == docs[:, :1], jnp.exp(cumulative), 0.0)
    leaving = jnp.where(docs == docs[:, TOK - 1 :], jnp.exp(ending - cumulative), 0.0)
    return cumulative, ending, entering, leaving


def local_states(
    x_hbm,
    dy_hbm,
    bc_hbm,
    step_hbm,
    docs_hbm,
    rate_ref,
    out_ref,
    sin_ref,
    sgr_ref,
    x_ref,
    dy_ref,
    bc_ref,
    step_ref,
    docs_ref,
    arrived,
):
    pairs = ((step_hbm, step_ref), (docs_hbm, docs_ref), (x_hbm, x_ref), (bc_hbm, bc_ref))
    pairs += ((dy_hbm, dy_ref),)
    copies = [
        pltpu.make_async_copy(source, target, arrived.at[i])
        for i, (source, target) in enumerate(pairs)
    ]
    for copy in copies:
        copy.start()
    table = head_table()
    rate = head_column(rate_ref)
    copies[0].wait()
    copies[1].wait()
    docs = docs_ref[...]
    _, ending, entering, leaving = decays(step_ref[0], rate, docs)
    leaving, entering = exact_right(leaving, table, TN), exact_right(entering, table, TN)
    copies[2].wait()
    scaled_in = (leaving * x_ref[0].astype(F32)).astype(BF16)
    sin_ref[...] = scaled_in
    copies[3].wait()
    closing = dot(bc_ref[0, 0], scaled_in, TN).astype(BF16)
    copies[4].wait()
    scaled_grad = (entering * dy_ref[0].astype(F32)).astype(BF16)
    sgr_ref[...] = scaled_grad
    opening = dot(bc_ref[0, 1], scaled_grad, TN).astype(BF16)
    passing = pieces(jnp.broadcast_to(jnp.exp(ending), (SSM_DEV, META)), 2)
    high, low = (dot(part, table, TN) for part in passing)
    row = iota((META, GROUP_COLS), 0)
    wide_docs = jnp.concatenate([docs.astype(F32), jnp.zeros((1, GROUP_COLS - TOK), F32)], axis=1)
    for g in range(SIDE):
        at = slice(g * GROUP_COLS, (g + 1) * GROUP_COLS)
        out_ref[g, :NS] = closing[:, at]
        out_ref[g, NS : 2 * NS] = opening[:, at]
        meta = jnp.where(row == 1, high[:, at], jnp.where(row == 2, low[:, at], 0.0))
        out_ref[g, 2 * NS :] = jnp.where(row == 0, wide_docs, meta).astype(BF16)


def pack(queries_ref, grads_ref, keyval_ref, docs_ref, out_ref, pair_ref, rows_ref, cots_ref):
    rows_ref[...] = queries_ref[0]
    cots_ref[...] = grads_ref[0]
    out_ref[:TOK] = queries_ref[0]
    out_ref[TOK : 2 * TOK] = grads_ref[0]
    out_ref[2 * TOK : 3 * TOK, :WIDTH] = keyval_ref[0, 0]
    out_ref[2 * TOK : 3 * TOK, WIDTH:] = keyval_ref[0, 1]
    docs = jnp.broadcast_to(docs_ref[...].astype(F32), (META, TOK)).astype(BF16)
    out_ref[3 * TOK :, :WIDTH] = docs
    out_ref[3 * TOK :, WIDTH:] = docs
    pair_ref[...] = out_ref[2 * TOK :]


def carried(ref, state_start, grad_start):
    first, last, through = [], [], []
    for p in range(SIDE):
        meta = ref[p, 2 * NS :].astype(F32)
        first.append(meta[:1, :1])
        last.append(meta[:1, TOK - 1 : TOK])
        through.append(jnp.where(first[p] == last[p], meta[1:2] + meta[2:3], 0.0))
    state_in, grad_in = [state_start], [grad_start]
    for p in range(SIDE):
        leaves = ref[p, :NS].astype(F32) + through[p] * state_in[p]
        if p < SIDE - 1:
            leaves = jnp.where(last[p] == first[p + 1], 1.0, 0.0) * leaves
        state_in.append(leaves)
    for p in range(SIDE - 1, -1, -1):
        leaves = ref[p, NS : 2 * NS].astype(F32) + through[p] * grad_in[0]
        if p > 0:
            leaves = jnp.where(first[p] == last[p - 1], 1.0, 0.0) * leaves
        grad_in.insert(0, leaves)
    return state_in, grad_in, first[0], last[-1]


def half_totals(half_ref, ref, out_ref):
    zero = jnp.zeros((NS, GROUP_COLS), F32)
    state_in, grad_in, first, last = carried(ref, zero, zero)
    upper = half_ref[0] > 0
    out_ref[:NS] = jnp.where(upper, grad_in[0], state_in[-1]).astype(BF16)
    edge = jnp.where(upper, first, last)
    out_ref[NS:] = jnp.broadcast_to(edge, (META, GROUP_COLS)).astype(BF16)


def entering_states(half_ref, ref, other_ref, out_ref):
    upper = half_ref[0] > 0
    first = ref[0, 2 * NS :].astype(F32)[:1, :1]
    last = ref[SIDE - 1, 2 * NS :].astype(F32)[:1, TOK - 1 : TOK]
    edge = other_ref[NS:].astype(F32)[:1, :1]
    meets = jnp.where(edge == jnp.where(upper, first, last), 1.0, 0.0)
    arrived = meets * other_ref[:NS].astype(F32)
    zero = jnp.zeros_like(arrived)
    state_in, grad_in, _, _ = carried(
        ref, jnp.where(upper, arrived, zero), jnp.where(upper, zero, arrived)
    )
    for p in range(SIDE):
        out_ref[p, :NS] = state_in[p].astype(BF16)
        out_ref[p, NS:] = grad_in[p + 1].astype(BF16)


def inside_shard(
    x_ref, dy_ref, bc_ref, step_ref, rate_ref, skip_ref, docs_ref, near_ref, shared_ref, aux_ref
):
    docs = docs_ref[...]
    rate = head_column(rate_ref)
    cumulative, ending, entering, leaving = decays(step_ref[0], rate, docs)
    log_decay = -step_ref[0] * rate
    aux_ref[1] = entering
    aux_ref[2] = leaving
    through = jnp.where(docs[:, :1] == docs[:, TOK - 1 :], jnp.exp(ending), 0.0)
    aux_ref[3] = jnp.broadcast_to(through, (SSM_DEV, TOK))
    aux_ref[4] = -rate
    aux_ref[5] = -step_ref[0]
    skip = jnp.sum(x_ref[0].astype(F32) * dy_ref[0].astype(F32), axis=0, keepdims=True)
    lanes, row = iota((TOK, COLS), 1), iota((TOK, COLS), 0)
    wide_table = jnp.where((lanes >= row * PD) & (lanes < (row + 1) * PD), 1.0, 0.0).astype(BF16)
    skips = exact_right(jnp.broadcast_to(skip, (SSM_DEV, COLS)), wide_table, NT, 3)
    aux_ref[6] = skips
    cumulative_t = exact_left(triangle(lambda t, s: s <= t), log_decay, NT, 3)
    writes, reads = bc_ref[0, 0], bc_ref[0, 1]
    wide = jnp.broadcast_to(docs.astype(F32), (SSM_DEV, TOK)).astype(BF16)
    docs_t = dot(triangle(lambda t, s: s == t), wide, NT)[:, :1]
    source, target = iota((TOK, TOK), 0), iota((TOK, TOK), 1)
    joined = (source <= target) & (docs_t == docs.astype(F32))
    affinity = dot(writes, reads, NT)
    after = triangle(lambda u, t: u >= t)
    paired_sum = jnp.zeros((TOK, TOK), F32)
    for h in range(SSM_DEV):
        at = slice(h * PD, (h + 1) * PD)
        x, dy = x_ref[0, :, at], dy_ref[0, :, at]
        spread = cumulative[h : h + 1] - cumulative_t[:, h : h + 1]
        weights = jnp.where(joined, jnp.exp(jnp.minimum(spread, 0.0)), 0.0)
        paired = weights * dot(x, dy, NT)
        near_ref[:, at] = dot((weights * affinity).astype(BF16), dy, NN) + skip_ref[h] * dy.astype(
            F32
        )
        paired_sum = paired_sum + paired
        reaching = exact_right(paired * affinity, after, NN)
        aux_ref[0, h : h + 1] = jnp.sum(
            jnp.where(source < target, reaching, 0.0), axis=0, keepdims=True
        )
    shared_ref[0] = exact_right(paired_sum, reads, NN)
    shared_ref[1] = exact_right(paired_sum, writes, TN)


def finish_ssm(
    scale,
    in_ref,
    x_ref,
    dy_ref,
    bc_ref,
    near_ref,
    shared_ref,
    aux_ref,
    sin_ref,
    sgr_ref,
    dx_ref,
    step_grad_ref,
    share_ref,
    params_ref,
):
    table = head_table()
    entering, leaving = aux_ref[1], aux_ref[2]
    leave_term = jnp.zeros((SSM_DEV, TOK), F32)
    enter_term = jnp.zeros((SSM_DEV, TOK), F32)
    across = jnp.zeros((SSM_DEV, 8), F32)
    write_grad, read_grad = shared_ref[0], shared_ref[1]
    for g in range(SIDE):
        at = slice(g * GROUP_COLS, (g + 1) * GROUP_COLS)
        part = table[:, at]
        state_in, grad_in = in_ref[g, :NS], in_ref[g, NS:]
        x, dy = x_ref[0, :, at].astype(F32), dy_ref[0, :, at].astype(F32)
        back = exact_right(leaving, part, TN) * dot(bc_ref[0, 0], grad_in, NN)
        ahead = exact_right(entering, part, TN) * dot(bc_ref[0, 1], state_in, NN)
        dx_ref[0, :, at] = (near_ref[:, at] + back).astype(BF16)
        leave_term += exact_left(part, back * x, NT)
        enter_term += exact_left(part, ahead * dy, NT)
        meeting = jnp.sum(state_in.astype(F32) * grad_in.astype(F32), axis=0, keepdims=True)
        across += exact_left(part, jnp.broadcast_to(meeting, (8, GROUP_COLS)), NT)
        write_grad += dot(sin_ref[:, at], grad_in, NT)
        read_grad += dot(sgr_ref[:, at], state_in, NT)
    log_grad = (
        aux_ref[0]
        + exact_right(enter_term, triangle(lambda u, t: u >= t), NN)
        + exact_right(leave_term, triangle(lambda s, t: s < t), NN)
        + aux_ref[3] * across[:, :1]
    )
    step_grad_ref[0] = aux_ref[4] * log_grad
    rates = exact_left(jnp.ones((8, TOK), BF16), aux_ref[5] * log_grad, NT, 3)
    peers, _, rows, _ = share_ref.shape
    for k in range(peers):
        at = slice(k * rows, (k + 1) * rows)
        share_ref[k, 0] = write_grad[at].astype(BF16)
        share_ref[k, 1] = read_grad[at].astype(BF16)
    rates = jnp.concatenate([rates[:1], jnp.zeros((1, TOK - SSM_DEV), F32)], axis=1)
    for row, value in enumerate((rates, aux_ref[6, :1])):
        params_ref[:, row : row + 1, :] = jnp.broadcast_to(
            (value * scale)[None], (params_ref.shape[0], 1, TOK)
        )


def attention(place_ref, *refs):
    dq_ref, dkv_ref, query_scr, grad_scr, key_scr, value_scr, doc_scr, total_scr = refs[SIDE:]
    half, mine = place_ref[0], place_ref[1]
    scaling = WIDTH ** (-0.5)

    for k in range(2):
        for step, ref in enumerate(refs[:SIDE]):
            shard_at = lax.bitwise_xor(half, k) * SIDE + lax.rem(mine + SIDE - step, SIDE)
            rows = pl.ds(pl.multiple_of(shard_at * TOK, TOK), TOK)
            query_scr[rows] = ref[k, :TOK]
            grad_scr[rows] = ref[k, TOK : 2 * TOK]
            key_scr[rows] = ref[k, 2 * TOK : 3 * TOK, :WIDTH]
            value_scr[rows] = ref[k, 2 * TOK : 3 * TOK, WIDTH:]
            doc_scr[:, rows] = ref[k, 3 * TOK :, :TOK].astype(F32)[:8]

    eye = triangle(lambda a, b: a == b)
    own_start = pl.multiple_of(mine * TOK, TOK)
    own_rows = pl.ds(own_start, TOK)
    own_keys, own_values = key_scr[own_rows], value_scr[own_rows]
    own_docs = doc_scr[:1, own_rows]
    key_lane = iota((TOK, WINDOW), 1)
    row_place = iota((TOK, WINDOW), 0)
    own_diff = iota((TOK, TOK), 1) - iota((TOK, TOK), 0)

    def rows_of(r, h):
        at, rows = slice(h * WIDTH, (h + 1) * WIDTH), pl.ds(pl.multiple_of(r * TOK, TOK), TOK)
        return query_scr[rows, at], grad_scr[rows, at]

    def shard(r, own):
        start = pl.multiple_of(jnp.maximum(r - SIDE, 0) * TOK, TOK)
        window = pl.ds(start, WINDOW)
        keys, values = key_scr[window], value_scr[window]
        row_docs = doc_scr[:, pl.ds(pl.multiple_of(r * TOK, TOK), TOK)].astype(BF16)
        docs_t = dot(eye, row_docs, NT)[:, :1]
        allowed = (key_lane + (start - r * TOK) <= row_place) & (docs_t == doc_scr[:1, window])
        own_allowed = (own_diff <= (r - mine) * TOK) & (docs_t == own_docs)
        for h in range(2):
            queries, grads = rows_of(r, h)
            scores = jnp.where(allowed, dot(queries, keys, NT) * scaling, NEGATIVE)
            top = jnp.max(scores, axis=1, keepdims=True)
            expos = jnp.where(allowed, jnp.exp(scores - top), 0.0)
            sums = jnp.sum(expos, axis=1, keepdims=True)
            dot_grads = dot(grads, values, NT)
            delta = jnp.sum(expos * dot_grads, axis=1, keepdims=True) / sums
            logsum = top + jnp.log(sums)
            if own:
                probs = jnp.where(allowed, jnp.exp(scores - logsum), 0.0).astype(BF16)
                dscore = (probs.astype(F32) * (dot_grads - delta)).astype(BF16)
                at = slice(h * WIDTH, (h + 1) * WIDTH)
                dq_ref[0, :, at] = (dot(dscore, keys, NN) * scaling).astype(BF16)
            scores = jnp.where(own_allowed, dot(queries, own_keys, NT) * scaling, NEGATIVE)
            probs = jnp.where(own_allowed, jnp.exp(scores - logsum), 0.0).astype(BF16)
            dot_grads = dot(grads, own_values, NT)
            dscore = (probs.astype(F32) * (dot_grads - delta)).astype(BF16)
            key_part = dot(dscore, queries, TN) * scaling
            value_part = dot(probs, grads, TN)
            if own and h == 0:
                total_scr[0] = key_part
                total_scr[1] = value_part
            else:
                total_scr[0] += key_part
                total_scr[1] += value_part

    shard(mine, True)
    lax.fori_loop(
        mine + 1,
        jnp.minimum(mine + SIDE, 2 * SIDE - 1) + 1,
        lambda r, _: (shard(r, False), 0)[1],
        0,
    )
    dkv_ref[0] = total_scr[...].astype(BF16)


def whole(count):
    return [pl.BlockSpec(memory_space=pltpu.VMEM)] * count


def scalars():
    return pl.BlockSpec(memory_space=pltpu.SMEM)


def params(megabytes=24):
    return pltpu.CompilerParams(vmem_limit_bytes=megabytes << 20)


def shape(dims, dtype):
    return jax.ShapeDtypeStruct(dims, dtype)


def body(
    queries, keyval, attn_grad, doc_ids, ssm_in, bc_pair, step_size, decay_rate, skip_gain, ssm_grad
):
    mine = lax.axis_index("ctx")
    half = mine // SIDE
    place = jnp.stack([half, mine]).astype(jnp.int32)
    peers = lax.axis_size("head")
    everyone = lax.axis_size("dp") * lax.axis_size("ctx")
    sides = [list(range(SIDE)), list(range(SIDE, 2 * SIDE))]
    across = [(i, i ^ SIDE) for i in range(2 * SIDE)]

    half_ring = lax.axis_size("dp")

    def at_place(place_on_ring, x):
        return (place_on_ring % half_ring) * 2 * SIDE + (place_on_ring // half_ring) * SIDE + x

    def stops(k, sign):
        step = k - sign
        return k + half_ring, step % half_ring, k

    def leg(number, sign):
        return [
            (at_place(stops(k, sign)[number], x), at_place(stops(k, sign)[number + 1], x))
            for k in range(half_ring)
            for x in range(SIDE)
            if 0 <= k - sign < half_ring
        ]

    straight = [
        (at_place(k + half_ring, x), at_place(k, x))
        for k in sorted({0, half_ring - 1})
        for x in range(SIDE)
    ]
    at_start = lax.axis_index("dp") == 0

    def between(value):
        return lax.all_to_all(value, "ctx", 0, 0, axis_index_groups=sides, tiled=True)

    sent, scaled_in, scaled_grad = pl.pallas_call(
        local_states,
        out_shape=(
            shape((SIDE, STATE_ROWS, GROUP_COLS), BF16),
            shape((TOK, COLS), BF16),
            shape((TOK, COLS), BF16),
        ),
        in_specs=[pl.BlockSpec(memory_space=pltpu.HBM)] * 5 + [scalars()],
        out_specs=tuple(whole(3)),
        scratch_shapes=[
            pltpu.VMEM(ssm_in.shape, BF16),
            pltpu.VMEM(ssm_grad.shape, BF16),
            pltpu.VMEM(bc_pair.shape, BF16),
            pltpu.VMEM(step_size.shape, F32),
            pltpu.VMEM(doc_ids.shape, jnp.int32),
            pltpu.SemaphoreType.DMA((5,)),
        ],
        compiler_params=params(63),
        name="local_states",
    )(ssm_in, ssm_grad, bc_pair, step_size, doc_ids, decay_rate)
    received = between(sent)

    docs_after, _ = lax.optimization_barrier((doc_ids, sent))
    own, own_pair, own_rows, own_cots = pl.pallas_call(
        pack,
        out_shape=(
            shape((ATT_ROWS, 2 * WIDTH), BF16),
            shape((TOK + META, 2 * WIDTH), BF16),
            shape((TOK, 2 * WIDTH), BF16),
            shape((TOK, 2 * WIDTH), BF16),
        ),
        in_specs=whole(4),
        out_specs=tuple(whole(4)),
        compiler_params=params(),
        name="pack",
    )(queries, attn_grad, keyval, docs_after)
    ends = lax.ppermute(jnp.where(at_start, own_cots, own_rows), ("dp", "ctx"), straight)
    near_rows = lax.ppermute(own_rows, ("dp", "ctx"), leg(0, -1))
    near_cots = lax.ppermute(own_cots, ("dp", "ctx"), leg(0, 1))

    step_after, _ = lax.optimization_barrier((step_size, own))
    near, shared_near, aux = pl.pallas_call(
        inside_shard,
        out_shape=(
            shape((TOK, COLS), F32),
            shape((2, TOK, NS), F32),
            shape((7, SSM_DEV, TOK), F32),
        ),
        in_specs=whole(4) + [scalars(), scalars()] + whole(1),
        out_specs=tuple(whole(3)),
        compiler_params=params(),
        name="inside_shard",
        cost_estimate=pl.CostEstimate(flops=1 << 10, bytes_accessed=1 << 10, transcendentals=0),
    )(ssm_in, ssm_grad, bc_pair, step_after, decay_rate, skip_gain, doc_ids)

    received, aux = lax.optimization_barrier((received, aux))
    total = pl.pallas_call(
        half_totals,
        out_shape=shape((NS + META, GROUP_COLS), BF16),
        in_specs=[scalars()] + whole(1),
        out_specs=whole(1)[0],
        compiler_params=params(),
        name="half_totals",
    )(place, received)
    other_total = lax.ppermute(total, "ctx", across)
    own_pair, _ = lax.optimization_barrier((own_pair, total))
    other_pair = lax.ppermute(own_pair, "ctx", across)

    def round_side(value, step):
        turn = [(i, (i & SIDE) | ((i + step) % SIDE)) for i in range(2 * SIDE)]
        return lax.ppermute(value, "ctx", turn)

    rows_above = lax.ppermute(near_rows, ("dp", "ctx"), leg(1, -1))
    cots_above = lax.ppermute(near_cots, ("dp", "ctx"), leg(1, 1))
    above = (rows_above, cots_above, ends)
    entering = pl.pallas_call(
        entering_states,
        out_shape=shape((SIDE, 2 * NS, GROUP_COLS), BF16),
        in_specs=[scalars()] + whole(2),
        out_specs=whole(1)[0],
        compiler_params=params(),
        name="entering_states",
    )(place, received, other_total)
    entered = between(entering)

    above, other_pair, _ = lax.optimization_barrier((above, other_pair, entering))
    rows_above, cots_above, ends = above
    none = jnp.zeros_like(ends)
    rows_above = rows_above + jnp.where(at_start, none, ends)
    cots_above = cots_above + jnp.where(at_start, ends, none)
    other = jnp.concatenate([rows_above, cots_above, other_pair])
    halves = jnp.stack([own, other])
    shards = [halves] + [round_side(halves, step) for step in range(1, SIDE)]

    near, _ = lax.optimization_barrier((near, halves))
    scale = 1.0 / math.sqrt(everyone * TOK * PD)
    input_grad, step_grad, share, both = pl.pallas_call(
        functools.partial(finish_ssm, scale),
        out_shape=(
            shape((1, TOK, COLS), BF16),
            shape((1, SSM_DEV, TOK), F32),
            shape((peers, 2, TOK // peers, NS), BF16),
            shape((everyone, 2, TOK), F32),
        ),
        in_specs=whole(9),
        out_specs=tuple(whole(4)),
        compiler_params=params(),
        name="finish_ssm",
    )(entered, ssm_in, ssm_grad, bc_pair, near, shared_near, aux, scaled_in, scaled_grad)
    shares = lax.all_to_all(share, "head", 0, 0, tiled=True)
    both, shares = lax.optimization_barrier((both, shares))
    everywhere = lax.all_to_all(both, ("dp", "ctx"), 0, 0, tiled=True)

    shards, _ = lax.optimization_barrier((shards, both))
    query_grad, keyval_grad = pl.pallas_call(
        attention,
        out_shape=(shape((1, TOK, 2 * WIDTH), BF16), shape((1, 2, TOK, WIDTH), BF16)),
        in_specs=[scalars()] + whole(SIDE),
        out_specs=tuple(whole(2)),
        scratch_shapes=[
            pltpu.VMEM((2 * SIDE * TOK, 2 * WIDTH), BF16),
            pltpu.VMEM((2 * SIDE * TOK, 2 * WIDTH), BF16),
            pltpu.VMEM((2 * SIDE * TOK, WIDTH), BF16),
            pltpu.VMEM((2 * SIDE * TOK, WIDTH), BF16),
            pltpu.VMEM((8, 2 * SIDE * TOK), F32),
            pltpu.VMEM((2, TOK, WIDTH), F32),
        ],
        compiler_params=params(),
        name="attention",
        cost_estimate=pl.CostEstimate(flops=2 << 30, bytes_accessed=4 << 20, transcendentals=1 << 20),
    )(place, *shards)

    shares, query_grad = lax.optimization_barrier((shares, query_grad))
    shared_grad = jnp.sum(shares.astype(F32), axis=0)[None]
    everywhere, shared_grad = lax.optimization_barrier((everywhere, shared_grad))
    param_grads = jnp.sum(everywhere, axis=0)[:, :SSM_DEV]
    return (query_grad, keyval_grad, input_grad, shared_grad, step_grad, param_grads)


def solution(mesh):
    placed = (
        P("dp", "ctx", "head"),
        P("dp", None, "ctx", "head"),
        P("dp", "ctx", "head"),
        P("dp", "ctx"),
        P("dp", "ctx", "head"),
        P("dp", None, "ctx", None),
        P("dp", "head", "ctx"),
        P("head"),
        P("head"),
        P("dp", "ctx", "head"),
    )
    return jax.shard_map(
        body,
        mesh=mesh,
        in_specs=placed,
        out_specs=(
            P("dp", "ctx", "head"),
            P("dp", None, "ctx", "head"),
            P("dp", "ctx", "head"),
            P("dp", None, ("ctx", "head"), None),
            P("dp", "head", "ctx"),
            P(None, "head"),
        ),
        check_vma=False,
    )
```

```python
import functools
import math

import jax
import jax.numpy as jnp
from jax import lax
from jax.experimental import pallas as pl
from jax.experimental.pallas import tpu as pltpu
from jax.sharding import PartitionSpec as P

TOK = 128
WIDTH = 128
PD = 64
NS = 128
SSM_DEV = 16
COLS = SSM_DEV * PD
SIDE = 4
GROUP_COLS = COLS // SIDE
WINDOW = 5 * TOK
META = 16
STATE_ROWS = 2 * NS + META
ATT_ROWS = 3 * TOK + META
NEGATIVE = -1e30
F32 = jnp.float32
BF16 = jnp.bfloat16

NN = (((1,), (0,)), ((), ()))
NT = (((1,), (1,)), ((), ()))
TN = (((0,), (0,)), ((), ()))


def dot(a, b, dims):
    return lax.dot_general(a, b, dims, preferred_element_type=F32)


def pieces(value, count):
    out = []
    for _ in range(count):
        part = value.astype(BF16)
        out.append(part)
        value = value - part.astype(F32)
    return out


def exact_right(value, fixed, dims, count=2):
    return sum(dot(part, fixed, dims) for part in pieces(value, count))


def exact_left(fixed, value, dims, count=2):
    return sum(dot(fixed, part, dims) for part in pieces(value, count))


def iota(shape, dim):
    return lax.broadcasted_iota(jnp.int32, shape, dim)


def head_table(rows=SSM_DEV):
    lanes, row = iota((rows, COLS), 1), iota((rows, COLS), 0)
    return jnp.where((lanes >= row * PD) & (lanes < (row + 1) * PD), 1.0, 0.0).astype(BF16)


def triangle(keep):
    return jnp.where(keep(iota((TOK, TOK), 0), iota((TOK, TOK), 1)), 1.0, 0.0).astype(BF16)


def head_column(ref):
    row = iota((SSM_DEV, TOK), 0)
    out = jnp.zeros((SSM_DEV, TOK), F32)
    for h in range(SSM_DEV):
        out = jnp.where(row == h, ref[h], out)
    return out


def decays(step, rate, docs):
    cumulative = exact_right(-step * rate, triangle(lambda s, t: s <= t), NN, 3)
    ending = cumulative[:, TOK - 1 :]
    entering = jnp.where(docs == docs[:, :1], jnp.exp(cumulative), 0.0)
    leaving = jnp.where(docs == docs[:, TOK - 1 :], jnp.exp(ending - cumulative), 0.0)
    return cumulative, ending, entering, leaving


def local_states(
    x_hbm,
    dy_hbm,
    bc_hbm,
    step_hbm,
    docs_hbm,
    rate_ref,
    out_ref,
    sin_ref,
    sgr_ref,
    x_ref,
    dy_ref,
    bc_ref,
    step_ref,
    docs_ref,
    arrived,
):
    pairs = ((step_hbm, step_ref), (docs_hbm, docs_ref), (x_hbm, x_ref), (bc_hbm, bc_ref))
    pairs += ((dy_hbm, dy_ref),)
    copies = [
        pltpu.make_async_copy(source, target, arrived.at[i])
        for i, (source, target) in enumerate(pairs)
    ]
    for copy in copies:
        copy.start()
    table = head_table()
    rate = head_column(rate_ref)
    copies[0].wait()
    copies[1].wait()
    docs = docs_ref[...]
    _, ending, entering, leaving = decays(step_ref[0], rate, docs)
    leaving, entering = exact_right(leaving, table, TN), exact_right(entering, table, TN)
    copies[2].wait()
    scaled_in = (leaving * x_ref[0].astype(F32)).astype(BF16)
    sin_ref[...] = scaled_in
    copies[3].wait()
    closing = dot(bc_ref[0, 0], scaled_in, TN).astype(BF16)
    copies[4].wait()
    scaled_grad = (entering * dy_ref[0].astype(F32)).astype(BF16)
    sgr_ref[...] = scaled_grad
    opening = dot(bc_ref[0, 1], scaled_grad, TN).astype(BF16)
    passing = pieces(jnp.broadcast_to(jnp.exp(ending), (SSM_DEV, META)), 2)
    high, low = (dot(part, table, TN) for part in passing)
    row = iota((META, GROUP_COLS), 0)
    wide_docs = jnp.concatenate([docs.astype(F32), jnp.zeros((1, GROUP_COLS - TOK), F32)], axis=1)
    for g in range(SIDE):
        at = slice(g * GROUP_COLS, (g + 1) * GROUP_COLS)
        out_ref[g, :NS] = closing[:, at]
        out_ref[g, NS : 2 * NS] = opening[:, at]
        meta = jnp.where(row == 1, high[:, at], jnp.where(row == 2, low[:, at], 0.0))
        out_ref[g, 2 * NS :] = jnp.where(row == 0, wide_docs, meta).astype(BF16)


def pack(queries_ref, grads_ref, keyval_ref, docs_ref, out_ref, pair_ref, rows_ref, cots_ref):
    rows_ref[...] = queries_ref[0]
    cots_ref[...] = grads_ref[0]
    out_ref[:TOK] = queries_ref[0]
    out_ref[TOK : 2 * TOK] = grads_ref[0]
    out_ref[2 * TOK : 3 * TOK, :WIDTH] = keyval_ref[0, 0]
    out_ref[2 * TOK : 3 * TOK, WIDTH:] = keyval_ref[0, 1]
    docs = jnp.broadcast_to(docs_ref[...].astype(F32), (META, TOK)).astype(BF16)
    out_ref[3 * TOK :, :WIDTH] = docs
    out_ref[3 * TOK :, WIDTH:] = docs
    pair_ref[...] = out_ref[2 * TOK :]


def carried(ref, state_start, grad_start):
    first, last, through = [], [], []
    for p in range(SIDE):
        meta = ref[p, 2 * NS :].astype(F32)
        first.append(meta[:1, :1])
        last.append(meta[:1, TOK - 1 : TOK])
        through.append(jnp.where(first[p] == last[p], meta[1:2] + meta[2:3], 0.0))
    state_in, grad_in = [state_start], [grad_start]
    for p in range(SIDE):
        leaves = ref[p, :NS].astype(F32) + through[p] * state_in[p]
        if p < SIDE - 1:
            leaves = jnp.where(last[p] == first[p + 1], 1.0, 0.0) * leaves
        state_in.append(leaves)
    for p in range(SIDE - 1, -1, -1):
        leaves = ref[p, NS : 2 * NS].astype(F32) + through[p] * grad_in[0]
        if p > 0:
            leaves = jnp.where(first[p] == last[p - 1], 1.0, 0.0) * leaves
        grad_in.insert(0, leaves)
    return state_in, grad_in, first[0], last[-1]


def half_totals(half_ref, ref, out_ref):
    zero = jnp.zeros((NS, GROUP_COLS), F32)
    state_in, grad_in, first, last = carried(ref, zero, zero)
    upper = half_ref[0] > 0
    out_ref[:NS] = jnp.where(upper, grad_in[0], state_in[-1]).astype(BF16)
    edge = jnp.where(upper, first, last)
    out_ref[NS:] = jnp.broadcast_to(edge, (META, GROUP_COLS)).astype(BF16)


def entering_states(half_ref, ref, other_ref, out_ref):
    upper = half_ref[0] > 0
    first = ref[0, 2 * NS :].astype(F32)[:1, :1]
    last = ref[SIDE - 1, 2 * NS :].astype(F32)[:1, TOK - 1 : TOK]
    edge = other_ref[NS:].astype(F32)[:1, :1]
    meets = jnp.where(edge == jnp.where(upper, first, last), 1.0, 0.0)
    arrived = meets * other_ref[:NS].astype(F32)
    zero = jnp.zeros_like(arrived)
    state_in, grad_in, _, _ = carried(
        ref, jnp.where(upper, arrived, zero), jnp.where(upper, zero, arrived)
    )
    for p in range(SIDE):
        out_ref[p, :NS] = state_in[p].astype(BF16)
        out_ref[p, NS:] = grad_in[p + 1].astype(BF16)


def inside_shard(
    x_ref, dy_ref, bc_ref, step_ref, rate_ref, skip_ref, docs_ref, near_ref, shared_ref, aux_ref
):
    docs = docs_ref[...]
    rate = head_column(rate_ref)
    cumulative, ending, entering, leaving = decays(step_ref[0], rate, docs)
    log_decay = -step_ref[0] * rate
    aux_ref[1] = entering
    aux_ref[2] = leaving
    through = jnp.where(docs[:, :1] == docs[:, TOK - 1 :], jnp.exp(ending), 0.0)
    aux_ref[3] = jnp.broadcast_to(through, (SSM_DEV, TOK))
    aux_ref[4] = -rate
    aux_ref[5] = -step_ref[0]
    skip = jnp.sum(x_ref[0].astype(F32) * dy_ref[0].astype(F32), axis=0, keepdims=True)
    lanes, row = iota((TOK, COLS), 1), iota((TOK, COLS), 0)
    wide_table = jnp.where((lanes >= row * PD) & (lanes < (row + 1) * PD), 1.0, 0.0).astype(BF16)
    skips = exact_right(jnp.broadcast_to(skip, (SSM_DEV, COLS)), wide_table, NT, 3)
    aux_ref[6] = skips
    cumulative_t = exact_left(triangle(lambda t, s: s <= t), log_decay, NT, 3)
    writes, reads = bc_ref[0, 0], bc_ref[0, 1]
    wide = jnp.broadcast_to(docs.astype(F32), (SSM_DEV, TOK)).astype(BF16)
    docs_t = dot(triangle(lambda t, s: s == t), wide, NT)[:, :1]
    source, target = iota((TOK, TOK), 0), iota((TOK, TOK), 1)
    joined = (source <= target) & (docs_t == docs.astype(F32))
    affinity = dot(writes, reads, NT)
    after = triangle(lambda u, t: u >= t)
    paired_sum = jnp.zeros((TOK, TOK), F32)
    for h in range(SSM_DEV):
        at = slice(h * PD, (h + 1) * PD)
        x, dy = x_ref[0, :, at], dy_ref[0, :, at]
        spread = cumulative[h : h + 1] - cumulative_t[:, h : h + 1]
        weights = jnp.where(joined, jnp.exp(jnp.minimum(spread, 0.0)), 0.0)
        paired = weights * dot(x, dy, NT)
        near_ref[:, at] = dot((weights * affinity).astype(BF16), dy, NN) + skip_ref[h] * dy.astype(
            F32
        )
        paired_sum = paired_sum + paired
        reaching = exact_right(paired * affinity, after, NN)
        aux_ref[0, h : h + 1] = jnp.sum(
            jnp.where(source < target, reaching, 0.0), axis=0, keepdims=True
        )
    shared_ref[0] = exact_right(paired_sum, reads, NN)
    shared_ref[1] = exact_right(paired_sum, writes, TN)


def finish_ssm(
    scale,
    in_ref,
    x_ref,
    dy_ref,
    bc_ref,
    near_ref,
    shared_ref,
    aux_ref,
    sin_ref,
    sgr_ref,
    dx_ref,
    step_grad_ref,
    share_ref,
    params_ref,
):
    table = head_table()
    entering, leaving = aux_ref[1], aux_ref[2]
    leave_term = jnp.zeros((SSM_DEV, TOK), F32)
    enter_term = jnp.zeros((SSM_DEV, TOK), F32)
    across = jnp.zeros((SSM_DEV, 8), F32)
    write_grad, read_grad = shared_ref[0], shared_ref[1]
    for g in range(SIDE):
        at = slice(g * GROUP_COLS, (g + 1) * GROUP_COLS)
        part = table[:, at]
        state_in, grad_in = in_ref[g, :NS], in_ref[g, NS:]
        x, dy = x_ref[0, :, at].astype(F32), dy_ref[0, :, at].astype(F32)
        back = exact_right(leaving, part, TN) * dot(bc_ref[0, 0], grad_in, NN)
        ahead = exact_right(entering, part, TN) * dot(bc_ref[0, 1], state_in, NN)
        dx_ref[0, :, at] = (near_ref[:, at] + back).astype(BF16)
        leave_term += exact_left(part, back * x, NT)
        enter_term += exact_left(part, ahead * dy, NT)
        meeting = jnp.sum(state_in.astype(F32) * grad_in.astype(F32), axis=0, keepdims=True)
        across += exact_left(part, jnp.broadcast_to(meeting, (8, GROUP_COLS)), NT)
        write_grad += dot(sin_ref[:, at], grad_in, NT)
        read_grad += dot(sgr_ref[:, at], state_in, NT)
    log_grad = (
        aux_ref[0]
        + exact_right(enter_term, triangle(lambda u, t: u >= t), NN)
        + exact_right(leave_term, triangle(lambda s, t: s < t), NN)
        + aux_ref[3] * across[:, :1]
    )
    step_grad_ref[0] = aux_ref[4] * log_grad
    rates = exact_left(jnp.ones((8, TOK), BF16), aux_ref[5] * log_grad, NT, 3)
    peers, _, rows, _ = share_ref.shape
    for k in range(peers):
        at = slice(k * rows, (k + 1) * rows)
        share_ref[k, 0] = write_grad[at].astype(BF16)
        share_ref[k, 1] = read_grad[at].astype(BF16)
    rates = jnp.concatenate([rates[:1], jnp.zeros((1, TOK - SSM_DEV), F32)], axis=1)
    for row, value in enumerate((rates, aux_ref[6, :1])):
        params_ref[:, row : row + 1, :] = jnp.broadcast_to(
            (value * scale)[None], (params_ref.shape[0], 1, TOK)
        )


def attention(place_ref, *refs):
    dq_ref, dkv_ref, query_scr, grad_scr, key_scr, value_scr, doc_scr, total_scr = refs[SIDE:]
    half, mine = place_ref[0], place_ref[1]
    scaling = WIDTH ** (-0.5)

    for k in range(2):
        for step, ref in enumerate(refs[:SIDE]):
            shard_at = lax.bitwise_xor(half, k) * SIDE + lax.rem(mine + SIDE - step, SIDE)
            rows = pl.ds(pl.multiple_of(shard_at * TOK, TOK), TOK)
            query_scr[rows] = ref[k, :TOK]
            grad_scr[rows] = ref[k, TOK : 2 * TOK]
            key_scr[rows] = ref[k, 2 * TOK : 3 * TOK, :WIDTH]
            value_scr[rows] = ref[k, 2 * TOK : 3 * TOK, WIDTH:]
            doc_scr[:, rows] = ref[k, 3 * TOK :, :TOK].astype(F32)[:8]

    eye = triangle(lambda a, b: a == b)
    own_start = pl.multiple_of(mine * TOK, TOK)
    own_rows = pl.ds(own_start, TOK)
    own_keys, own_values = key_scr[own_rows], value_scr[own_rows]
    own_docs = doc_scr[:1, own_rows]
    key_lane = iota((TOK, WINDOW), 1)
    row_place = iota((TOK, WINDOW), 0)
    own_diff = iota((TOK, TOK), 1) - iota((TOK, TOK), 0)

    def rows_of(r, h):
        at, rows = slice(h * WIDTH, (h + 1) * WIDTH), pl.ds(pl.multiple_of(r * TOK, TOK), TOK)
        return query_scr[rows, at], grad_scr[rows, at]

    def shard(r, own):
        start = pl.multiple_of(jnp.maximum(r - SIDE, 0) * TOK, TOK)
        window = pl.ds(start, WINDOW)
        keys, values = key_scr[window], value_scr[window]
        row_docs = doc_scr[:, pl.ds(pl.multiple_of(r * TOK, TOK), TOK)].astype(BF16)
        docs_t = dot(eye, row_docs, NT)[:, :1]
        allowed = (key_lane + (start - r * TOK) <= row_place) & (docs_t == doc_scr[:1, window])
        own_allowed = (own_diff <= (r - mine) * TOK) & (docs_t == own_docs)
        for h in range(2):
            queries, grads = rows_of(r, h)
            scores = jnp.where(allowed, dot(queries, keys, NT) * scaling, NEGATIVE)
            top = jnp.max(scores, axis=1, keepdims=True)
            expos = jnp.where(allowed, jnp.exp(scores - top), 0.0)
            sums = jnp.sum(expos, axis=1, keepdims=True)
            dot_grads = dot(grads, values, NT)
            delta = jnp.sum(expos * dot_grads, axis=1, keepdims=True) / sums
            logsum = top + jnp.log(sums)
            if own:
                probs = jnp.where(allowed, jnp.exp(scores - logsum), 0.0).astype(BF16)
                dscore = (probs.astype(F32) * (dot_grads - delta)).astype(BF16)
                at = slice(h * WIDTH, (h + 1) * WIDTH)
                dq_ref[0, :, at] = (dot(dscore, keys, NN) * scaling).astype(BF16)
            scores = jnp.where(own_allowed, dot(queries, own_keys, NT) * scaling, NEGATIVE)
            probs = jnp.where(own_allowed, jnp.exp(scores - logsum), 0.0).astype(BF16)
            dot_grads = dot(grads, own_values, NT)
            dscore = (probs.astype(F32) * (dot_grads - delta)).astype(BF16)
            key_part = dot(dscore, queries, TN) * scaling
            value_part = dot(probs, grads, TN)
            if own and h == 0:
                total_scr[0] = key_part
                total_scr[1] = value_part
            else:
                total_scr[0] += key_part
                total_scr[1] += value_part

    shard(mine, True)
    last_doc = jnp.max(own_docs, axis=1, keepdims=True)
    places = iota((1, 2 * SIDE * TOK), 1).astype(F32)
    last_place = jnp.max(jnp.where(doc_scr[:1] == last_doc, places, 0.0)).astype(jnp.int32)
    stop = jnp.minimum(jnp.minimum(last_place // TOK, mine + SIDE), 2 * SIDE - 1) + 1
    lax.fori_loop(mine + 1, stop, lambda r, _: (shard(r, False), 0)[1], 0)
    dkv_ref[0] = total_scr[...].astype(BF16)


def whole(count):
    return [pl.BlockSpec(memory_space=pltpu.VMEM)] * count


def scalars():
    return pl.BlockSpec(memory_space=pltpu.SMEM)


def params(megabytes=24):
    return pltpu.CompilerParams(vmem_limit_bytes=megabytes << 20)


def shape(dims, dtype):
    return jax.ShapeDtypeStruct(dims, dtype)


def body(
    queries, keyval, attn_grad, doc_ids, ssm_in, bc_pair, step_size, decay_rate, skip_gain, ssm_grad
):
    mine = lax.axis_index("ctx")
    half = mine // SIDE
    place = jnp.stack([half, mine]).astype(jnp.int32)
    peers = lax.axis_size("head")
    everyone = lax.axis_size("dp") * lax.axis_size("ctx")
    sides = [list(range(SIDE)), list(range(SIDE, 2 * SIDE))]
    across = [(i, i ^ SIDE) for i in range(2 * SIDE)]

    half_ring = lax.axis_size("dp")

    def at_place(place_on_ring, x):
        return (place_on_ring % half_ring) * 2 * SIDE + (place_on_ring // half_ring) * SIDE + x

    def stops(k, sign):
        step = k - sign
        return k + half_ring, step % half_ring, k

    def leg(number, sign):
        return [
            (at_place(stops(k, sign)[number], x), at_place(stops(k, sign)[number + 1], x))
            for k in range(half_ring)
            for x in range(SIDE)
            if 0 <= k - sign < half_ring
        ]

    straight = [
        (at_place(k + half_ring, x), at_place(k, x))
        for k in sorted({0, half_ring - 1})
        for x in range(SIDE)
    ]
    at_start = lax.axis_index("dp") == 0

    def between(value):
        return lax.all_to_all(value, "ctx", 0, 0, axis_index_groups=sides, tiled=True)

    sent, scaled_in, scaled_grad = pl.pallas_call(
        local_states,
        out_shape=(
            shape((SIDE, STATE_ROWS, GROUP_COLS), BF16),
            shape((TOK, COLS), BF16),
            shape((TOK, COLS), BF16),
        ),
        in_specs=[pl.BlockSpec(memory_space=pltpu.HBM)] * 5 + [scalars()],
        out_specs=tuple(whole(3)),
        scratch_shapes=[
            pltpu.VMEM(ssm_in.shape, BF16),
            pltpu.VMEM(ssm_grad.shape, BF16),
            pltpu.VMEM(bc_pair.shape, BF16),
            pltpu.VMEM(step_size.shape, F32),
            pltpu.VMEM(doc_ids.shape, jnp.int32),
            pltpu.SemaphoreType.DMA((5,)),
        ],
        compiler_params=params(63),
        name="local_states",
    )(ssm_in, ssm_grad, bc_pair, step_size, doc_ids, decay_rate)
    received = between(sent)

    docs_after, _ = lax.optimization_barrier((doc_ids, sent))
    own, own_pair, own_rows, own_cots = pl.pallas_call(
        pack,
        out_shape=(
            shape((ATT_ROWS, 2 * WIDTH), BF16),
            shape((TOK + META, 2 * WIDTH), BF16),
            shape((TOK, 2 * WIDTH), BF16),
            shape((TOK, 2 * WIDTH), BF16),
        ),
        in_specs=whole(4),
        out_specs=tuple(whole(4)),
        compiler_params=params(),
        name="pack",
    )(queries, attn_grad, keyval, docs_after)
    ends = lax.ppermute(jnp.where(at_start, own_cots, own_rows), ("dp", "ctx"), straight)
    near_rows = lax.ppermute(own_rows, ("dp", "ctx"), leg(0, -1))
    near_cots = lax.ppermute(own_cots, ("dp", "ctx"), leg(0, 1))

    step_after, _ = lax.optimization_barrier((step_size, own))
    near, shared_near, aux = pl.pallas_call(
        inside_shard,
        out_shape=(
            shape((TOK, COLS), F32),
            shape((2, TOK, NS), F32),
            shape((7, SSM_DEV, TOK), F32),
        ),
        in_specs=whole(4) + [scalars(), scalars()] + whole(1),
        out_specs=tuple(whole(3)),
        compiler_params=params(),
        name="inside_shard",
        cost_estimate=pl.CostEstimate(flops=1 << 10, bytes_accessed=1 << 10, transcendentals=0),
    )(ssm_in, ssm_grad, bc_pair, step_after, decay_rate, skip_gain, doc_ids)

    received, aux = lax.optimization_barrier((received, aux))
    total = pl.pallas_call(
        half_totals,
        out_shape=shape((NS + META, GROUP_COLS), BF16),
        in_specs=[scalars()] + whole(1),
        out_specs=whole(1)[0],
        compiler_params=params(),
        name="half_totals",
    )(place, received)
    other_total = lax.ppermute(total, "ctx", across)
    own_pair, _ = lax.optimization_barrier((own_pair, total))
    other_pair = lax.ppermute(own_pair, "ctx", across)

    def round_side(value, step):
        turn = [(i, (i & SIDE) | ((i + step) % SIDE)) for i in range(2 * SIDE)]
        return lax.ppermute(value, "ctx", turn)

    rows_above = lax.ppermute(near_rows, ("dp", "ctx"), leg(1, -1))
    cots_above = lax.ppermute(near_cots, ("dp", "ctx"), leg(1, 1))
    above = (rows_above, cots_above, ends)
    entering = pl.pallas_call(
        entering_states,
        out_shape=shape((SIDE, 2 * NS, GROUP_COLS), BF16),
        in_specs=[scalars()] + whole(2),
        out_specs=whole(1)[0],
        compiler_params=params(),
        name="entering_states",
    )(place, received, other_total)
    entered = between(entering)

    above, other_pair, _ = lax.optimization_barrier((above, other_pair, entering))
    rows_above, cots_above, ends = above
    none = jnp.zeros_like(ends)
    rows_above = rows_above + jnp.where(at_start, none, ends)
    cots_above = cots_above + jnp.where(at_start, ends, none)
    other = jnp.concatenate([rows_above, cots_above, other_pair])
    halves = jnp.stack([own, other])
    shards = [halves] + [round_side(halves, step) for step in range(1, SIDE)]

    near, _ = lax.optimization_barrier((near, halves))
    scale = 1.0 / math.sqrt(everyone * TOK * PD)
    input_grad, step_grad, share, both = pl.pallas_call(
        functools.partial(finish_ssm, scale),
        out_shape=(
            shape((1, TOK, COLS), BF16),
            shape((1, SSM_DEV, TOK), F32),
            shape((peers, 2, TOK // peers, NS), BF16),
            shape((everyone, 2, TOK), F32),
        ),
        in_specs=whole(9),
        out_specs=tuple(whole(4)),
        compiler_params=params(),
        name="finish_ssm",
    )(entered, ssm_in, ssm_grad, bc_pair, near, shared_near, aux, scaled_in, scaled_grad)
    shares = lax.all_to_all(share, "head", 0, 0, tiled=True)
    both, shares = lax.optimization_barrier((both, shares))
    order = [
        at_place((k + half_ring) % (2 * half_ring), x) for k in range(2 * half_ring) for x in range(SIDE)
    ]
    everywhere = lax.all_to_all(
        both, ("dp", "ctx"), 0, 0, axis_index_groups=[order], tiled=True
    )

    shards, _ = lax.optimization_barrier((shards, both))
    query_grad, keyval_grad = pl.pallas_call(
        attention,
        out_shape=(shape((1, TOK, 2 * WIDTH), BF16), shape((1, 2, TOK, WIDTH), BF16)),
        in_specs=[scalars()] + whole(SIDE),
        out_specs=tuple(whole(2)),
        scratch_shapes=[
            pltpu.VMEM((2 * SIDE * TOK, 2 * WIDTH), BF16),
            pltpu.VMEM((2 * SIDE * TOK, 2 * WIDTH), BF16),
            pltpu.VMEM((2 * SIDE * TOK, WIDTH), BF16),
            pltpu.VMEM((2 * SIDE * TOK, WIDTH), BF16),
            pltpu.VMEM((8, 2 * SIDE * TOK), F32),
            pltpu.VMEM((2, TOK, WIDTH), F32),
        ],
        compiler_params=params(),
        name="attention",
        cost_estimate=pl.CostEstimate(flops=2 << 30, bytes_accessed=4 << 20, transcendentals=1 << 20),
    )(place, *shards)

    shares, query_grad = lax.optimization_barrier((shares, query_grad))
    shared_grad = jnp.sum(shares.astype(F32), axis=0)[None]
    everywhere, shared_grad = lax.optimization_barrier((everywhere, shared_grad))
    param_grads = jnp.sum(everywhere, axis=0)[:, :SSM_DEV]
    return (query_grad, keyval_grad, input_grad, shared_grad, step_grad, param_grads)


def solution(mesh):
    placed = (
        P("dp", "ctx", "head"),
        P("dp", None, "ctx", "head"),
        P("dp", "ctx", "head"),
        P("dp", "ctx"),
        P("dp", "ctx", "head"),
        P("dp", None, "ctx", None),
        P("dp", "head", "ctx"),
        P("head"),
        P("head"),
        P("dp", "ctx", "head"),
    )
    return jax.shard_map(
        body,
        mesh=mesh,
        in_specs=placed,
        out_specs=(
            P("dp", "ctx", "head"),
            P("dp", None, "ctx", "head"),
            P("dp", "ctx", "head"),
            P("dp", None, ("ctx", "head"), None),
            P("dp", "head", "ctx"),
            P(None, "head"),
        ),
        check_vma=False,
    )
```

```python
import functools
import math

import jax
import jax.numpy as jnp
from jax import lax
from jax.experimental import pallas as pl
from jax.experimental.pallas import tpu as pltpu
from jax.sharding import PartitionSpec as P

TOK = 128
WIDTH = 128
PD = 64
NS = 128
SSM_DEV = 16
COLS = SSM_DEV * PD
SIDE = 4
GROUP_COLS = COLS // SIDE
WINDOW = 5 * TOK
META = 16
TURN = 2
STATE_ROWS = 2 * NS + META
ATT_ROWS = 3 * TOK + META
NEGATIVE = -1e30
F32 = jnp.float32
BF16 = jnp.bfloat16

NN = (((1,), (0,)), ((), ()))
NT = (((1,), (1,)), ((), ()))
TN = (((0,), (0,)), ((), ()))


def dot(a, b, dims):
    return lax.dot_general(a, b, dims, preferred_element_type=F32)


def pieces(value, count):
    out = []
    for _ in range(count):
        part = value.astype(BF16)
        out.append(part)
        value = value - part.astype(F32)
    return out


def exact_right(value, fixed, dims, count=2):
    return sum(dot(part, fixed, dims) for part in pieces(value, count))


def exact_left(fixed, value, dims, count=2):
    return sum(dot(fixed, part, dims) for part in pieces(value, count))


def iota(shape, dim):
    return lax.broadcasted_iota(jnp.int32, shape, dim)


def head_table(rows=SSM_DEV):
    lanes, row = iota((rows, COLS), 1), iota((rows, COLS), 0)
    return jnp.where((lanes >= row * PD) & (lanes < (row + 1) * PD), 1.0, 0.0).astype(BF16)


def triangle(keep):
    return jnp.where(keep(iota((TOK, TOK), 0), iota((TOK, TOK), 1)), 1.0, 0.0).astype(BF16)


def head_column(ref):
    row = iota((SSM_DEV, TOK), 0)
    out = jnp.zeros((SSM_DEV, TOK), F32)
    for h in range(SSM_DEV):
        out = jnp.where(row == h, ref[h], out)
    return out


def decays(step, rate, docs):
    cumulative = exact_right(-step * rate, triangle(lambda s, t: s <= t), NN, 3)
    ending = cumulative[:, TOK - 1 :]
    entering = jnp.where(docs == docs[:, :1], jnp.exp(cumulative), 0.0)
    leaving = jnp.where(docs == docs[:, TOK - 1 :], jnp.exp(ending - cumulative), 0.0)
    return cumulative, ending, entering, leaving


def local_states(
    x_hbm,
    dy_hbm,
    bc_hbm,
    step_hbm,
    docs_hbm,
    rate_ref,
    out_ref,
    sin_ref,
    sgr_ref,
    x_ref,
    dy_ref,
    bc_ref,
    step_ref,
    docs_ref,
    arrived,
):
    pairs = ((step_hbm, step_ref), (docs_hbm, docs_ref), (x_hbm, x_ref), (bc_hbm, bc_ref))
    pairs += ((dy_hbm, dy_ref),)
    copies = [
        pltpu.make_async_copy(source, target, arrived.at[i])
        for i, (source, target) in enumerate(pairs)
    ]
    for copy in copies:
        copy.start()
    table = head_table()
    rate = head_column(rate_ref)
    copies[0].wait()
    copies[1].wait()
    docs = docs_ref[...]
    _, ending, entering, leaving = decays(step_ref[0], rate, docs)
    leaving, entering = exact_right(leaving, table, TN), exact_right(entering, table, TN)
    copies[2].wait()
    scaled_in = (leaving * x_ref[0].astype(F32)).astype(BF16)
    sin_ref[...] = scaled_in
    copies[3].wait()
    closing = dot(bc_ref[0, 0], scaled_in, TN).astype(BF16)
    copies[4].wait()
    scaled_grad = (entering * dy_ref[0].astype(F32)).astype(BF16)
    sgr_ref[...] = scaled_grad
    opening = dot(bc_ref[0, 1], scaled_grad, TN).astype(BF16)
    passing = pieces(jnp.broadcast_to(jnp.exp(ending), (SSM_DEV, META)), 2)
    high, low = (dot(part, table, TN) for part in passing)
    row = iota((META, GROUP_COLS), 0)
    wide_docs = jnp.concatenate([docs.astype(F32), jnp.zeros((1, GROUP_COLS - TOK), F32)], axis=1)
    for g in range(SIDE):
        at = slice(g * GROUP_COLS, (g + 1) * GROUP_COLS)
        out_ref[g ^ TURN, :NS] = closing[:, at]
        out_ref[g ^ TURN, NS : 2 * NS] = opening[:, at]
        meta = jnp.where(row == 1, high[:, at], jnp.where(row == 2, low[:, at], 0.0))
        out_ref[g ^ TURN, 2 * NS :] = jnp.where(row == 0, wide_docs, meta).astype(BF16)


def pack(queries_ref, grads_ref, keyval_ref, docs_ref, out_ref, pair_ref, rows_ref, cots_ref):
    rows_ref[...] = queries_ref[0]
    cots_ref[...] = grads_ref[0]
    out_ref[:TOK] = queries_ref[0]
    out_ref[TOK : 2 * TOK] = grads_ref[0]
    out_ref[2 * TOK : 3 * TOK, :WIDTH] = keyval_ref[0, 0]
    out_ref[2 * TOK : 3 * TOK, WIDTH:] = keyval_ref[0, 1]
    docs = jnp.broadcast_to(docs_ref[...].astype(F32), (META, TOK)).astype(BF16)
    out_ref[3 * TOK :, :WIDTH] = docs
    out_ref[3 * TOK :, WIDTH:] = docs
    pair_ref[...] = out_ref[2 * TOK :]


def carried(ref, state_start, grad_start):
    first, last, through = [], [], []
    for p in range(SIDE):
        meta = ref[p ^ TURN, 2 * NS :].astype(F32)
        first.append(meta[:1, :1])
        last.append(meta[:1, TOK - 1 : TOK])
        through.append(jnp.where(first[p] == last[p], meta[1:2] + meta[2:3], 0.0))
    state_in, grad_in = [state_start], [grad_start]
    for p in range(SIDE):
        leaves = ref[p ^ TURN, :NS].astype(F32) + through[p] * state_in[p]
        if p < SIDE - 1:
            leaves = jnp.where(last[p] == first[p + 1], 1.0, 0.0) * leaves
        state_in.append(leaves)
    for p in range(SIDE - 1, -1, -1):
        leaves = ref[p ^ TURN, NS : 2 * NS].astype(F32) + through[p] * grad_in[0]
        if p > 0:
            leaves = jnp.where(first[p] == last[p - 1], 1.0, 0.0) * leaves
        grad_in.insert(0, leaves)
    return state_in, grad_in, first[0], last[-1]


def half_totals(half_ref, ref, out_ref):
    zero = jnp.zeros((NS, GROUP_COLS), F32)
    state_in, grad_in, first, last = carried(ref, zero, zero)
    upper = half_ref[0] > 0
    out_ref[:NS] = jnp.where(upper, grad_in[0], state_in[-1]).astype(BF16)
    edge = jnp.where(upper, first, last)
    out_ref[NS:] = jnp.broadcast_to(edge, (META, GROUP_COLS)).astype(BF16)


def entering_states(half_ref, ref, other_ref, out_ref):
    upper = half_ref[0] > 0
    first = ref[TURN, 2 * NS :].astype(F32)[:1, :1]
    last = ref[(SIDE - 1) ^ TURN, 2 * NS :].astype(F32)[:1, TOK - 1 : TOK]
    edge = other_ref[NS:].astype(F32)[:1, :1]
    meets = jnp.where(edge == jnp.where(upper, first, last), 1.0, 0.0)
    arrived = meets * other_ref[:NS].astype(F32)
    zero = jnp.zeros_like(arrived)
    state_in, grad_in, _, _ = carried(
        ref, jnp.where(upper, arrived, zero), jnp.where(upper, zero, arrived)
    )
    for p in range(SIDE):
        out_ref[p ^ TURN, :NS] = state_in[p].astype(BF16)
        out_ref[p ^ TURN, NS:] = grad_in[p + 1].astype(BF16)


def inside_shard(
    x_ref, dy_ref, bc_ref, step_ref, rate_ref, skip_ref, docs_ref, near_ref, shared_ref, aux_ref
):
    docs = docs_ref[...]
    rate = head_column(rate_ref)
    cumulative, ending, entering, leaving = decays(step_ref[0], rate, docs)
    log_decay = -step_ref[0] * rate
    aux_ref[1] = entering
    aux_ref[2] = leaving
    through = jnp.where(docs[:, :1] == docs[:, TOK - 1 :], jnp.exp(ending), 0.0)
    aux_ref[3] = jnp.broadcast_to(through, (SSM_DEV, TOK))
    aux_ref[4] = -rate
    aux_ref[5] = -step_ref[0]
    skip = jnp.sum(x_ref[0].astype(F32) * dy_ref[0].astype(F32), axis=0, keepdims=True)
    lanes, row = iota((TOK, COLS), 1), iota((TOK, COLS), 0)
    wide_table = jnp.where((lanes >= row * PD) & (lanes < (row + 1) * PD), 1.0, 0.0).astype(BF16)
    skips = exact_right(jnp.broadcast_to(skip, (SSM_DEV, COLS)), wide_table, NT, 3)
    aux_ref[6] = skips
    cumulative_t = exact_left(triangle(lambda t, s: s <= t), log_decay, NT, 3)
    writes, reads = bc_ref[0, 0], bc_ref[0, 1]
    wide = jnp.broadcast_to(docs.astype(F32), (SSM_DEV, TOK)).astype(BF16)
    docs_t = dot(triangle(lambda t, s: s == t), wide, NT)[:, :1]
    source, target = iota((TOK, TOK), 0), iota((TOK, TOK), 1)
    joined = (source <= target) & (docs_t == docs.astype(F32))
    affinity = dot(writes, reads, NT)
    after = triangle(lambda u, t: u >= t)
    paired_sum = jnp.zeros((TOK, TOK), F32)
    for h in range(SSM_DEV):
        at = slice(h * PD, (h + 1) * PD)
        x, dy = x_ref[0, :, at], dy_ref[0, :, at]
        spread = cumulative[h : h + 1] - cumulative_t[:, h : h + 1]
        weights = jnp.where(joined, jnp.exp(jnp.minimum(spread, 0.0)), 0.0)
        paired = weights * dot(x, dy, NT)
        near_ref[:, at] = dot((weights * affinity).astype(BF16), dy, NN) + skip_ref[h] * dy.astype(
            F32
        )
        paired_sum = paired_sum + paired
        reaching = exact_right(paired * affinity, after, NN)
        aux_ref[0, h : h + 1] = jnp.sum(
            jnp.where(source < target, reaching, 0.0), axis=0, keepdims=True
        )
    shared_ref[0] = exact_right(paired_sum, reads, NN)
    shared_ref[1] = exact_right(paired_sum, writes, TN)


def finish_ssm(
    scale,
    in_ref,
    x_ref,
    dy_ref,
    bc_ref,
    near_ref,
    shared_ref,
    aux_ref,
    sin_ref,
    sgr_ref,
    dx_ref,
    step_grad_ref,
    share_ref,
    params_ref,
):
    table = head_table()
    entering, leaving = aux_ref[1], aux_ref[2]
    leave_term = jnp.zeros((SSM_DEV, TOK), F32)
    enter_term = jnp.zeros((SSM_DEV, TOK), F32)
    across = jnp.zeros((SSM_DEV, 8), F32)
    write_grad, read_grad = shared_ref[0], shared_ref[1]
    for g in range(SIDE):
        at = slice(g * GROUP_COLS, (g + 1) * GROUP_COLS)
        part = table[:, at]
        state_in, grad_in = in_ref[g ^ TURN, :NS], in_ref[g ^ TURN, NS:]
        x, dy = x_ref[0, :, at].astype(F32), dy_ref[0, :, at].astype(F32)
        back = exact_right(leaving, part, TN) * dot(bc_ref[0, 0], grad_in, NN)
        ahead = exact_right(entering, part, TN) * dot(bc_ref[0, 1], state_in, NN)
        dx_ref[0, :, at] = (near_ref[:, at] + back).astype(BF16)
        leave_term += exact_left(part, back * x, NT)
        enter_term += exact_left(part, ahead * dy, NT)
        meeting = jnp.sum(state_in.astype(F32) * grad_in.astype(F32), axis=0, keepdims=True)
        across += exact_left(part, jnp.broadcast_to(meeting, (8, GROUP_COLS)), NT)
        write_grad += dot(sin_ref[:, at], grad_in, NT)
        read_grad += dot(sgr_ref[:, at], state_in, NT)
    log_grad = (
        aux_ref[0]
        + exact_right(enter_term, triangle(lambda u, t: u >= t), NN)
        + exact_right(leave_term, triangle(lambda s, t: s < t), NN)
        + aux_ref[3] * across[:, :1]
    )
    step_grad_ref[0] = aux_ref[4] * log_grad
    rates = exact_left(jnp.ones((8, TOK), BF16), aux_ref[5] * log_grad, NT, 3)
    peers, _, rows, _ = share_ref.shape
    for k in range(peers):
        at = slice(k * rows, (k + 1) * rows)
        share_ref[k, 0] = write_grad[at].astype(BF16)
        share_ref[k, 1] = read_grad[at].astype(BF16)
    rates = jnp.concatenate([rates[:1], jnp.zeros((1, TOK - SSM_DEV), F32)], axis=1)
    for row, value in enumerate((rates, aux_ref[6, :1])):
        params_ref[:, row : row + 1, :] = jnp.broadcast_to(
            (value * scale)[None], (params_ref.shape[0], 1, TOK)
        )


def attention(place_ref, *refs):
    dq_ref, dkv_ref, query_scr, grad_scr, key_scr, value_scr, doc_scr, total_scr = refs[SIDE:]
    half, mine = place_ref[0], place_ref[1]
    scaling = WIDTH ** (-0.5)

    for k in range(2):
        for step, ref in enumerate(refs[:SIDE]):
            shard_at = lax.bitwise_xor(half, k) * SIDE + lax.rem(mine + SIDE - step, SIDE)
            rows = pl.ds(pl.multiple_of(shard_at * TOK, TOK), TOK)
            query_scr[rows] = ref[k, :TOK]
            grad_scr[rows] = ref[k, TOK : 2 * TOK]
            key_scr[rows] = ref[k, 2 * TOK : 3 * TOK, :WIDTH]
            value_scr[rows] = ref[k, 2 * TOK : 3 * TOK, WIDTH:]
            doc_scr[:, rows] = ref[k, 3 * TOK :, :TOK].astype(F32)[:8]

    eye = triangle(lambda a, b: a == b)
    own_start = pl.multiple_of(mine * TOK, TOK)
    own_rows = pl.ds(own_start, TOK)
    own_keys, own_values = key_scr[own_rows], value_scr[own_rows]
    own_docs = doc_scr[:1, own_rows]
    key_lane = iota((TOK, WINDOW), 1)
    row_place = iota((TOK, WINDOW), 0)
    own_diff = iota((TOK, TOK), 1) - iota((TOK, TOK), 0)

    def rows_of(r, h):
        at, rows = slice(h * WIDTH, (h + 1) * WIDTH), pl.ds(pl.multiple_of(r * TOK, TOK), TOK)
        return query_scr[rows, at], grad_scr[rows, at]

    def shard(r, own):
        start = pl.multiple_of(jnp.maximum(r - SIDE, 0) * TOK, TOK)
        window = pl.ds(start, WINDOW)
        keys, values = key_scr[window], value_scr[window]
        row_docs = doc_scr[:, pl.ds(pl.multiple_of(r * TOK, TOK), TOK)].astype(BF16)
        docs_t = dot(eye, row_docs, NT)[:, :1]
        allowed = (key_lane + (start - r * TOK) <= row_place) & (docs_t == doc_scr[:1, window])
        own_allowed = (own_diff <= (r - mine) * TOK) & (docs_t == own_docs)
        for h in range(2):
            queries, grads = rows_of(r, h)
            scores = jnp.where(allowed, dot(queries, keys, NT) * scaling, NEGATIVE)
            top = jnp.max(scores, axis=1, keepdims=True)
            expos = jnp.where(allowed, jnp.exp(scores - top), 0.0)
            sums = jnp.sum(expos, axis=1, keepdims=True)
            dot_grads = dot(grads, values, NT)
            delta = jnp.sum(expos * dot_grads, axis=1, keepdims=True) / sums
            logsum = top + jnp.log(sums)
            if own:
                probs = jnp.where(allowed, jnp.exp(scores - logsum), 0.0).astype(BF16)
                dscore = (probs.astype(F32) * (dot_grads - delta)).astype(BF16)
                at = slice(h * WIDTH, (h + 1) * WIDTH)
                dq_ref[0, :, at] = (dot(dscore, keys, NN) * scaling).astype(BF16)
            scores = jnp.where(own_allowed, dot(queries, own_keys, NT) * scaling, NEGATIVE)
            probs = jnp.where(own_allowed, jnp.exp(scores - logsum), 0.0).astype(BF16)
            dot_grads = dot(grads, own_values, NT)
            dscore = (probs.astype(F32) * (dot_grads - delta)).astype(BF16)
            key_part = dot(dscore, queries, TN) * scaling
            value_part = dot(probs, grads, TN)
            if own and h == 0:
                total_scr[0] = key_part
                total_scr[1] = value_part
            else:
                total_scr[0] += key_part
                total_scr[1] += value_part

    shard(mine, True)
    last_doc = jnp.max(own_docs, axis=1, keepdims=True)
    places = iota((1, 2 * SIDE * TOK), 1).astype(F32)
    last_place = jnp.max(jnp.where(doc_scr[:1] == last_doc, places, 0.0)).astype(jnp.int32)
    stop = jnp.minimum(jnp.minimum(last_place // TOK, mine + SIDE), 2 * SIDE - 1) + 1
    lax.fori_loop(mine + 1, stop, lambda r, _: (shard(r, False), 0)[1], 0)
    dkv_ref[0] = total_scr[...].astype(BF16)


def whole(count):
    return [pl.BlockSpec(memory_space=pltpu.VMEM)] * count


def scalars():
    return pl.BlockSpec(memory_space=pltpu.SMEM)


def params(megabytes=24):
    return pltpu.CompilerParams(vmem_limit_bytes=megabytes << 20)


def shape(dims, dtype):
    return jax.ShapeDtypeStruct(dims, dtype)


def body(
    queries, keyval, attn_grad, doc_ids, ssm_in, bc_pair, step_size, decay_rate, skip_gain, ssm_grad
):
    mine = lax.axis_index("ctx")
    half = mine // SIDE
    place = jnp.stack([half, mine]).astype(jnp.int32)
    peers = lax.axis_size("head")
    everyone = lax.axis_size("dp") * lax.axis_size("ctx")
    sides = [[start + (rank ^ TURN) for rank in range(SIDE)] for start in (0, SIDE)]
    across = [(i, i ^ SIDE) for i in range(2 * SIDE)]

    half_ring = lax.axis_size("dp")

    def at_place(place_on_ring, x):
        return (place_on_ring % half_ring) * 2 * SIDE + (place_on_ring // half_ring) * SIDE + x

    def stops(k, sign):
        step = k - sign
        return k + half_ring, step % half_ring, k

    def leg(number, sign):
        return [
            (at_place(stops(k, sign)[number], x), at_place(stops(k, sign)[number + 1], x))
            for k in range(half_ring)
            for x in range(SIDE)
            if 0 <= k - sign < half_ring
        ]

    straight = [
        (at_place(k + half_ring, x), at_place(k, x))
        for k in sorted({0, half_ring - 1})
        for x in range(SIDE)
    ]
    at_start = lax.axis_index("dp") == 0

    def between(value):
        return lax.all_to_all(value, "ctx", 0, 0, axis_index_groups=sides, tiled=True)

    sent, scaled_in, scaled_grad = pl.pallas_call(
        local_states,
        out_shape=(
            shape((SIDE, STATE_ROWS, GROUP_COLS), BF16),
            shape((TOK, COLS), BF16),
            shape((TOK, COLS), BF16),
        ),
        in_specs=[pl.BlockSpec(memory_space=pltpu.HBM)] * 5 + [scalars()],
        out_specs=tuple(whole(3)),
        scratch_shapes=[
            pltpu.VMEM(ssm_in.shape, BF16),
            pltpu.VMEM(ssm_grad.shape, BF16),
            pltpu.VMEM(bc_pair.shape, BF16),
            pltpu.VMEM(step_size.shape, F32),
            pltpu.VMEM(doc_ids.shape, jnp.int32),
            pltpu.SemaphoreType.DMA((5,)),
        ],
        compiler_params=params(63),
        name="local_states",
    )(ssm_in, ssm_grad, bc_pair, step_size, doc_ids, decay_rate)
    received = between(sent)

    docs_after, _ = lax.optimization_barrier((doc_ids, sent))
    own, own_pair, own_rows, own_cots = pl.pallas_call(
        pack,
        out_shape=(
            shape((ATT_ROWS, 2 * WIDTH), BF16),
            shape((TOK + META, 2 * WIDTH), BF16),
            shape((TOK, 2 * WIDTH), BF16),
            shape((TOK, 2 * WIDTH), BF16),
        ),
        in_specs=whole(4),
        out_specs=tuple(whole(4)),
        compiler_params=params(),
        name="pack",
    )(queries, attn_grad, keyval, docs_after)
    ends = lax.ppermute(jnp.where(at_start, own_cots, own_rows), ("dp", "ctx"), straight)
    near_rows = lax.ppermute(own_rows, ("dp", "ctx"), leg(0, -1))
    near_cots = lax.ppermute(own_cots, ("dp", "ctx"), leg(0, 1))

    step_after, _ = lax.optimization_barrier((step_size, own))
    near, shared_near, aux = pl.pallas_call(
        inside_shard,
        out_shape=(
            shape((TOK, COLS), F32),
            shape((2, TOK, NS), F32),
            shape((7, SSM_DEV, TOK), F32),
        ),
        in_specs=whole(4) + [scalars(), scalars()] + whole(1),
        out_specs=tuple(whole(3)),
        compiler_params=params(),
        name="inside_shard",
        cost_estimate=pl.CostEstimate(flops=1 << 10, bytes_accessed=1 << 10, transcendentals=0),
    )(ssm_in, ssm_grad, bc_pair, step_after, decay_rate, skip_gain, doc_ids)

    received, aux = lax.optimization_barrier((received, aux))
    total = pl.pallas_call(
        half_totals,
        out_shape=shape((NS + META, GROUP_COLS), BF16),
        in_specs=[scalars()] + whole(1),
        out_specs=whole(1)[0],
        compiler_params=params(),
        name="half_totals",
    )(place, received)
    other_total = lax.ppermute(total, "ctx", across)
    own_pair, _ = lax.optimization_barrier((own_pair, total))
    other_pair = lax.ppermute(own_pair, "ctx", across)

    def round_side(value, step):
        turn = [(i, (i & SIDE) | ((i + step) % SIDE)) for i in range(2 * SIDE)]
        return lax.ppermute(value, "ctx", turn)

    rows_above = lax.ppermute(near_rows, ("dp", "ctx"), leg(1, -1))
    cots_above = lax.ppermute(near_cots, ("dp", "ctx"), leg(1, 1))
    above = (rows_above, cots_above, ends)
    entering = pl.pallas_call(
        entering_states,
        out_shape=shape((SIDE, 2 * NS, GROUP_COLS), BF16),
        in_specs=[scalars()] + whole(2),
        out_specs=whole(1)[0],
        compiler_params=params(),
        name="entering_states",
    )(place, received, other_total)
    entered = between(entering)

    above, other_pair, _ = lax.optimization_barrier((above, other_pair, entering))
    rows_above, cots_above, ends = above
    none = jnp.zeros_like(ends)
    rows_above = rows_above + jnp.where(at_start, none, ends)
    cots_above = cots_above + jnp.where(at_start, ends, none)
    other = jnp.concatenate([rows_above, cots_above, other_pair])
    halves = jnp.stack([own, other])
    shards = [halves] + [round_side(halves, step) for step in range(1, SIDE)]

    near, _ = lax.optimization_barrier((near, halves))
    scale = 1.0 / math.sqrt(everyone * TOK * PD)
    input_grad, step_grad, share, both = pl.pallas_call(
        functools.partial(finish_ssm, scale),
        out_shape=(
            shape((1, TOK, COLS), BF16),
            shape((1, SSM_DEV, TOK), F32),
            shape((peers, 2, TOK // peers, NS), BF16),
            shape((everyone, 2, TOK), F32),
        ),
        in_specs=whole(9),
        out_specs=tuple(whole(4)),
        compiler_params=params(),
        name="finish_ssm",
    )(entered, ssm_in, ssm_grad, bc_pair, near, shared_near, aux, scaled_in, scaled_grad)
    shares = lax.all_to_all(share, "head", 0, 0, tiled=True)
    both, shares = lax.optimization_barrier((both, shares))
    order = [
        at_place((k + half_ring) % (2 * half_ring), x) for k in range(2 * half_ring) for x in range(SIDE)
    ]
    everywhere = lax.all_to_all(
        both, ("dp", "ctx"), 0, 0, axis_index_groups=[order], tiled=True
    )

    shards, _ = lax.optimization_barrier((shards, both))
    query_grad, keyval_grad = pl.pallas_call(
        attention,
        out_shape=(shape((1, TOK, 2 * WIDTH), BF16), shape((1, 2, TOK, WIDTH), BF16)),
        in_specs=[scalars()] + whole(SIDE),
        out_specs=tuple(whole(2)),
        scratch_shapes=[
            pltpu.VMEM((2 * SIDE * TOK, 2 * WIDTH), BF16),
            pltpu.VMEM((2 * SIDE * TOK, 2 * WIDTH), BF16),
            pltpu.VMEM((2 * SIDE * TOK, WIDTH), BF16),
            pltpu.VMEM((2 * SIDE * TOK, WIDTH), BF16),
            pltpu.VMEM((8, 2 * SIDE * TOK), F32),
            pltpu.VMEM((2, TOK, WIDTH), F32),
        ],
        compiler_params=params(),
        name="attention",
        cost_estimate=pl.CostEstimate(flops=2 << 30, bytes_accessed=4 << 20, transcendentals=1 << 20),
    )(place, *shards)

    shares, query_grad = lax.optimization_barrier((shares, query_grad))
    shared_grad = jnp.sum(shares.astype(F32), axis=0)[None]
    everywhere, shared_grad = lax.optimization_barrier((everywhere, shared_grad))
    param_grads = jnp.sum(everywhere, axis=0)[:, :SSM_DEV]
    return (query_grad, keyval_grad, input_grad, shared_grad, step_grad, param_grads)


def solution(mesh):
    placed = (
        P("dp", "ctx", "head"),
        P("dp", None, "ctx", "head"),
        P("dp", "ctx", "head"),
        P("dp", "ctx"),
        P("dp", "ctx", "head"),
        P("dp", None, "ctx", None),
        P("dp", "head", "ctx"),
        P("head"),
        P("head"),
        P("dp", "ctx", "head"),
    )
    return jax.shard_map(
        body,
        mesh=mesh,
        in_specs=placed,
        out_specs=(
            P("dp", "ctx", "head"),
            P("dp", None, "ctx", "head"),
            P("dp", "ctx", "head"),
            P("dp", None, ("ctx", "head"), None),
            P("dp", "head", "ctx"),
            P(None, "head"),
        ),
        check_vma=False,
    )
```
